32 devices in a mesh: band: 2 (over x), lev: 16 (over z, y, core).
Axes of the slice: x: 2, y: 2, z: 4, core: 2. Of those that a mesh axis runs over, the one named last changes fastest.
Arguments:
- tracer: float32 [64, 16, 16, 512], P(None, 'lev', 'band'), parts along dimension 2, may hold values from -6 to 6
- east_flow: float32 [16, 16, 512], P('lev', 'band'), parts along dimension 1, may hold values from -0.3 to 0.3
- north_flow: float32 [16, 16, 512], P('lev', 'band'), parts along dimension 1, may hold values from -0.3 to 0.3
- up_flow: float32 [16, 16, 512], P('lev', 'band'), parts along dimension 1, may hold values from -0.3 to 0.3
- diffusivity: float32 [16, 16, 512], P('lev', 'band'), parts along dimension 1, may hold values from 30 to 300
- thickness: float32 [16], replicated, may hold values from 1.5 to 4
- kmt: int32 [16, 512], P('band'), parts along dimension 0, may hold values from 0 to 16, as said below
- group: int32 [64], replicated, may hold values from 0 to 7, as said below
- group_rate: float32 [8, 16], replicated, may hold values from 0.02 to 0.4
Outputs:
- updated: float32 [64, 16, 16, 512], P(None, 'lev', 'band'), parts along dimension 2
The draws below stay inside these ranges and needn't reach their ends.
There are 2 independent parts, one for each index of `band`. The reference program is written for one: setup_inputs(seed, part) draws one part's arguments, and reference() takes and returns one part's arrays. A program takes and returns all parts, laid end to end along the dimension named above; an argument that names none is the same for every part. Nothing has to cross between parts.
Inputs may be any that keep to these rules, and one draw needn't show every extreme that they name: `kmt`: 0 marks land; some column has all 16 levels wet and some is land. Every group holds some tracers.
All inputs are finite; a program needn't handle non-finite values.
Results may differ from the reference program's by a relative error of at most 0.0003.
Values sent between devices are 32-bit elements; how exact they have to be, the bound alone decides.
No kernel may reach another device: no remote copies, remote signals or barrier semaphores. Data moves between devices by JAX's collectives and lax.ppermute only.
A program may use at most 256 MiB of HBM per device.

```python
import math
import jax
import jax.numpy as jnp
from jax import lax

NTR = 64
NGRP = 8
NY = 8
NX = 512
NZ = 16


def draw_kmt(key, part):
    key = jax.random.fold_in(key, 11)
    first, second, third = jax.random.split(key, 3)
    values = jax.random.randint(first, (NY * NX,), 0, NZ + 1)
    deep_spot = jax.random.randint(second, (), 0, NY * NX)
    land_spot = (deep_spot + 1 + jax.random.randint(third, (), 0, NY * NX - 1)) % (NY * NX)
    place = jnp.arange(NY * NX)
    values = jnp.where(place == deep_spot, NZ, values)
    values = jnp.where(place == land_spot, 0, values)
    return values.reshape(NY, NX).astype(jnp.int32)


def draw_group(key, part):
    key = jax.random.fold_in(key, 23)
    order = jax.random.permutation(key, NTR)
    return (order % NGRP).astype(jnp.int32)


def block_scale(key, extent, cuts, smallest, top_value):
    loudness = 1.0
    for position, parts in cuts:
        heights = jax.random.uniform(jax.random.fold_in(jax.random.fold_in(key, 6), position), (parts,), jnp.float32, smallest / len(cuts), top_value / len(cuts))
        loudness = loudness * jnp.repeat(jnp.exp(heights), extent[position] // parts).reshape((-1,) + (1,) * (len(extent) - 1 - position))
    return loudness


def centred(own_key, extent, spread, most, cuts=(), held_as=jnp.bfloat16):
    result = jax.random.normal(own_key, extent, jnp.float32) * spread
    if len(cuts) > 0:
        result = block_scale(own_key, extent, cuts, -0.22, 0.18) * result
    return jnp.clip(result, min=-most, max=most).astype(held_as)


def setup_inputs(seed: int = 0, part: int = 0) -> dict:
    splits = jax.random.split(jax.random.key(seed), 10)
    part_splits = jax.random.split(jax.random.fold_in(splits[9], part), 10)
    tracer = centred(part_splits[0], (NTR, NZ, NY, NX), 1.0, 6.0, ((1, 16),), jnp.float32)
    east_flow = jnp.clip(jax.random.uniform(part_splits[1], (NZ, NY, NX), jnp.float32, -0.3, 0.3) * block_scale(part_splits[1], (NZ, NY, NX), ((0, 16),), -0.4, 0.0), -0.3, 0.3)
    north_flow = jnp.clip(jax.random.uniform(part_splits[2], (NZ, NY, NX), jnp.float32, -0.3, 0.3) * block_scale(part_splits[2], (NZ, NY, NX), ((0, 16),), -0.4, 0.0), -0.3, 0.3)
    up_flow = jnp.clip(jax.random.uniform(part_splits[3], (NZ, NY, NX), jnp.float32, -0.3, 0.3) * block_scale(part_splits[3], (NZ, NY, NX), ((0, 16),), -0.4, 0.0), -0.3, 0.3)
    diffusivity = jnp.clip(jnp.exp(math.log(300.0) - 2.3025851 * jax.random.uniform(part_splits[4], (NZ, NY, NX), jnp.float32) ** block_scale(part_splits[4], (NZ, NY, NX), ((0, 16),), -0.2, 0.2)), 30.0, 300.0)
    thickness = jnp.clip(jnp.exp(jax.random.uniform(splits[5], (NZ,), jnp.float32, math.log(1.5), math.log(4.0))), 1.5, 4.0)
    kmt = draw_kmt(jax.random.fold_in(jax.random.fold_in(splits[9], part), 71), part)
    group = draw_group(jax.random.fold_in(splits[9], 71), part)
    group_rate = jnp.clip(jnp.exp(jax.random.uniform(splits[8], (NGRP, NZ), jnp.float32, math.log(0.02), math.log(0.4))), 0.02, 0.4)
    return dict(tracer=tracer, east_flow=east_flow, north_flow=north_flow, up_flow=up_flow, diffusivity=diffusivity, thickness=thickness, kmt=kmt, group=group, group_rate=group_rate)


def forward(carry, inputs):
    cprime, dprime = carry
    lower, diag, upper, rhs = inputs
    denom = diag - lower * cprime
    cnew = upper / denom
    dnew = (rhs - lower * dprime) / denom
    return (cnew, dnew), (cnew, dnew)


def backward(x_next, inputs):
    cprime, dprime = inputs
    value = dprime - cprime * x_next
    return value, value


def reference(tracer, east_flow, north_flow, up_flow, diffusivity, thickness, kmt, group, group_rate):
    f32 = jnp.float32
    level = jnp.arange(NZ, dtype=jnp.int32)
    wet = (level[:, None, None] < kmt[None]).astype(f32)
    wet_up = wet * jnp.concatenate([jnp.zeros((1, NY, NX), f32), wet[:-1]], 0)
    dz_prev = jnp.concatenate([thickness[:1], thickness[:-1]])
    dz3 = thickness[:, None, None]
    onehot = (group[:, None] == jnp.arange(NGRP, dtype=jnp.int32)[None]).astype(f32)
    rate = jnp.dot(onehot, group_rate, precision=lax.Precision.HIGHEST)
    east = east_flow[:, :, :-1] * wet[:, :, :-1] * wet[:, :, 1:]
    face_e = jnp.maximum(east, 0.0) * tracer[..., :-1] + jnp.minimum(east, 0.0) * tracer[..., 1:]
    zcol = jnp.zeros((NTR, NZ, NY, 1), f32)
    div_e = jnp.concatenate([face_e, zcol], 3) - jnp.concatenate([zcol, face_e], 3)
    north = north_flow[:, :-1, :] * wet[:, :-1, :] * wet[:, 1:, :]
    face_n = jnp.maximum(north, 0.0) * tracer[:, :, :-1] + jnp.minimum(north, 0.0) * tracer[:, :, 1:]
    zrow = jnp.zeros((NTR, NZ, 1, NX), f32)
    div_n = jnp.concatenate([face_n, zrow], 2) - jnp.concatenate([zrow, face_n], 2)
    zlev = jnp.zeros((NTR, 1, NY, NX), f32)
    c_above = jnp.concatenate([zlev, tracer[:, :-1]], 1)
    upward = up_flow * wet_up
    dz_min = jnp.minimum(dz_prev, thickness)[:, None, None]
    flux = dz_min * (jnp.maximum(upward, 0.0) * tracer + jnp.minimum(upward, 0.0) * c_above)
    flux_below = jnp.concatenate([flux[:, 1:], zlev], 1)
    star = wet * (tracer - div_e - div_n + (flux_below - flux) / dz3 - rate[:, :, None, None] * tracer)
    coeff = diffusivity * wet_up / (0.5 * (dz_prev + thickness))[:, None, None]
    coeff_next = jnp.concatenate([coeff[1:], jnp.zeros((1, NY, NX), f32)], 0)
    lower = -coeff / dz3
    upper = -coeff_next / dz3
    diag = 1.0 - lower - upper
    start = (jnp.zeros((NTR, NY, NX), f32), jnp.zeros((NTR, NY, NX), f32))
    rhs = jnp.moveaxis(star, 1, 0)
    _, (cps, dps) = lax.scan(forward, start, (lower, diag, upper, rhs))
    _, solved = lax.scan(backward, jnp.zeros((NTR, NY, NX), f32), (cps, dps), reverse=True)
    return jnp.moveaxis(solved, 0, 1)
```

```python
import functools

import jax
import jax.numpy as jnp
from jax import lax
from jax.experimental import pallas as pl
from jax.experimental.pallas import tpu as pltpu
from jax.sharding import PartitionSpec as P

LANES = 128
ROWS = 8
EAST, NORTH, UP, DIFF, EDGE, EXTRA = 0, 1, 2, 3, 4, 5
f32 = jnp.float32
VMEM_LIMIT = 32 * 1024 * 1024


def lanes_iota():
    return lax.broadcasted_iota(jnp.int32, (ROWS, LANES), 1)


def rows_iota():
    return lax.broadcasted_iota(jnp.int32, (ROWS, LANES), 0)


def pack_kernel(nb, tc, tpc, meta, tracer, east, north, up, diff, kmt, out):
    level = meta[0]
    lane = lanes_iota()
    wet = [
        (level < kmt[:, b * LANES : (b + 1) * LANES]).astype(f32) for b in range(nb)
    ]
    flow = [None]
    for b in range(1, nb):
        ends = east[0, :, b * LANES - LANES : b * LANES][:, LANES - 1 :]
        ends = ends * wet[b - 1][:, LANES - 1 :] * wet[b][:, :1]
        flow.append(jnp.broadcast_to(ends, (ROWS, LANES)))
    for c in range(tc):
        faces = [jnp.zeros((ROWS, LANES), f32) for _ in range(nb)]
        for t in range(tpc):
            tiles = [tracer[c * tpc + t, 0, :, b * LANES : (b + 1) * LANES] for b in range(nb)]
            for b in range(nb):
                out[b * tc + c, t] = tiles[b]
            for b in range(1, nb):
                west = pltpu.roll(tiles[b - 1], (2 * t + 1) % LANES, 1)
                here = pltpu.roll(tiles[b], 2 * t, 1) if t else tiles[b]
                face = jnp.maximum(flow[b], 0.0) * west + jnp.minimum(flow[b], 0.0) * here
                faces[b] = jnp.where(lane == 2 * t, face, faces[b])
        for b in range(nb):
            edge = faces[b]
            if b + 1 < nb:
                edge = edge - pltpu.roll(faces[b + 1], LANES - 1, 1)
            out[b * tc + c, tpc + EDGE] = edge
    for b in range(nb):
        cols = slice(b * LANES, (b + 1) * LANES)
        for c in range(tc):
            out[b * tc + c, tpc + EAST] = east[0, :, cols]
            out[b * tc + c, tpc + NORTH] = north[0, :, cols]
            out[b * tc + c, tpc + UP] = up[0, :, cols]
            out[b * tc + c, tpc + DIFF] = diff[0, :, cols]


def solve_kernel(
    half, tpc, meta, thickness, group, rates, got, kmt_all, across,
    f_out, cin_out, alpha_out, message,
):
    upper, block, chunk = meta[0], meta[1], meta[2]
    sign = 1.0 - 2.0 * upper.astype(f32)
    kmt = kmt_all[:, pl.ds(pl.multiple_of(block * LANES, LANES), LANES)]
    lane, row = lanes_iota(), rows_iota()
    ends = jnp.logical_or(lane == 0, lane == LANES - 1)
    first = jnp.where(upper == 1, 2 * half - 1, 0)
    step = 1 - 2 * upper

    def level_of(o):
        return first + step * o

    def slot_of(o):
        return jnp.where(upper == 1, half - 1 - o, o)

    zero = jnp.zeros((ROWS, LANES), f32)
    cin = tout = outer = add_mid = zero
    for o in range(half):
        k = level_of(o)
        slot = slot_of(o)
        dz, dz_next = thickness[k], thickness[level_of(o + 1)]
        wet = (k < kmt).astype(f32)
        wet_next = (level_of(o + 1) < kmt).astype(f32)
        if o + 1 < half:
            face = jnp.where(upper == 1, slot, slot_of(o + 1))
            w, g = got[face, tpc + UP], got[face, tpc + DIFF]
        else:
            w = jnp.where(upper == 1, got[0, tpc + UP], across[0])
            g = jnp.where(upper == 1, got[0, tpc + DIFF], across[1])
        open_face = wet * wet_next
        w = sign * w * open_face
        g = g * open_face / (0.5 * (dz + dz_next))
        dz_min = jnp.minimum(dz, dz_next)
        pos, neg = dz_min * jnp.maximum(w, 0.0), dz_min * jnp.minimum(w, 0.0)
        inner = -g / dz
        tin = pos / dz
        mid = wet + add_mid + neg / dz
        alpha = 1.0 / (1.0 - outer - inner - outer * cin)
        cin_new = inner * alpha
        east = got[slot, tpc + EAST] * wet * pltpu.roll(wet, LANES - 1, 1)
        east = jnp.where(lane == LANES - 1, 0.0, east)
        north = got[slot, tpc + NORTH] * wet * pltpu.roll(wet, ROWS - 1, 0)
        north = jnp.where(row == ROWS - 1, 0.0, north)
        e_pos, e_neg = jnp.maximum(east, 0.0), jnp.minimum(east, 0.0)
        n_pos, n_neg = jnp.maximum(north, 0.0), jnp.minimum(north, 0.0)
        edges = got[slot, tpc + EDGE]
        last = o + 1 == half
        prev_slot = slot_of(o - 1) if o else None
        next_slot = None if last else slot_of(o + 1)
        tout_next = -neg / dz_next
        outer_next = -g / dz_next

        def body(t, _, o=o, k=k, slot=slot, wet=wet, mid=mid, tin=tin, tout=tout, outer=outer,
                 alpha=alpha, e_pos=e_pos, e_neg=e_neg, n_pos=n_pos, n_neg=n_neg, edges=edges,
                 last=last, prev_slot=prev_slot, next_slot=next_slot, tout_next=tout_next,
                 outer_next=outer_next):
            c = got[slot, t]
            rate = rates[group[chunk * tpc + t], k]
            star = c * (mid - rate * wet)
            if o:
                star += tout * got[prev_slot, t]
            if not last:
                star += tin * got[next_slot, t]
            fe = e_pos * c + e_neg * pltpu.roll(c, LANES - 1, 1)
            fn = n_pos * c + n_neg * pltpu.roll(c, ROWS - 1, 0)
            star -= fe - pltpu.roll(fe, 1, 1)
            star -= fn - pltpu.roll(fn, 1, 0)
            star += jnp.where(ends, pltpu.roll(edges, (LANES - 2 * t) % LANES, 1), 0.0)
            if o:
                star -= outer * f_out[o - 1, t]
            f = alpha * star
            f_out[o, t] = f
            if last:
                message[t] = tout_next * c - outer_next * f
            return 0

        lax.fori_loop(0, tpc, body, 0, unroll=8)
        cin_out[o] = cin_new
        if last:
            alpha_out[0] = alpha
            alpha_out[1] = outer_next
            message[tpc] = alpha
        cin, tout, outer, add_mid = cin_new, tout_next, outer_next, -pos / dz_next


def back_kernel(half, tpc, meta, f_in, cin, alpha, sent, got, out):
    upper = meta[0]
    other = cin[half - 1] * got[tpc]
    scale = 1.0 / (1.0 - other * alpha[1])
    mine, theirs = scale * alpha[0], scale * other

    def body(t, _):
        x = f_in[half - 1, t] + (mine * got[t] - theirs * sent[t])
        out[jnp.where(upper == 1, 0, half - 1), t] = x
        for o in range(half - 2, -1, -1):
            x = f_in[o, t] - cin[o] * x
            out[jnp.where(upper == 1, half - 1 - o, o), t] = x
        return 0

    lax.fori_loop(0, tpc, body, 0, unroll=8)


def join_kernel(nb, tc, tpc, got, out):
    for b in range(nb):
        for c in range(tc):
            out[c * tpc : (c + 1) * tpc, 0, :, b * LANES : (b + 1) * LANES] = got[b * tc + c]


def shards(tracer, east_flow, north_flow, up_flow, diffusivity, thickness, kmt, group, group_rate):
    ntr, ldev, ny, nx = tracer.shape
    count = lax.axis_size("lev")
    half = count // 2
    nb = nx // LANES
    tc = half // nb
    tpc = ntr // tc
    assert ldev == 1 and ny == ROWS and nb * LANES == nx and tc * nb == half and tpc * tc == ntr
    index = lax.axis_index("lev").astype(jnp.int32)
    upper, rank = index // half, index % half
    meta = jnp.stack([upper, rank // tc, rank % tc, index])
    vm = pl.BlockSpec(memory_space=pltpu.VMEM)
    sm = pl.BlockSpec(memory_space=pltpu.SMEM)
    params = pltpu.CompilerParams(vmem_limit_bytes=VMEM_LIMIT)
    groups = [[h * half + i for i in range(half)] for h in range(2)]

    pieces = pl.pallas_call(
        functools.partial(pack_kernel, nb, tc, tpc),
        out_shape=jax.ShapeDtypeStruct((half, tpc + EXTRA, ROWS, LANES), f32),
        in_specs=[sm] + [vm] * 6,
        out_specs=vm,
        compiler_params=params,
        name="pack",
    )(index[None], tracer, east_flow, north_flow, up_flow, diffusivity, kmt)
    got = lax.all_to_all(pieces, "lev", 0, 0, axis_index_groups=groups, tiled=True)

    fields = jnp.concatenate([up_flow, diffusivity], 0)
    across = jnp.zeros((2, ROWS, LANES), f32)
    for r in range(half):
        cols = lax.slice_in_dim(fields, (r // tc) * LANES, (r // tc + 1) * LANES, axis=2)
        across = across + lax.ppermute(cols, "lev", [(half, r)])

    tile = (ROWS, LANES)
    f, cin, alpha, message = pl.pallas_call(
        functools.partial(solve_kernel, half, tpc),
        out_shape=(
            jax.ShapeDtypeStruct((half, tpc) + tile, f32),
            jax.ShapeDtypeStruct((half,) + tile, f32),
            jax.ShapeDtypeStruct((2,) + tile, f32),
            jax.ShapeDtypeStruct((tpc + 1,) + tile, f32),
        ),
        in_specs=[sm, sm, sm, sm, vm, vm, vm],
        out_specs=(vm, vm, vm, vm),
        compiler_params=params,
        name="solve",
    )(meta, thickness, group, group_rate, got, kmt, across)
    theirs = lax.ppermute(
        message, "lev", [(i, (i + half) % count) for i in range(count)]
    )
    solved = pl.pallas_call(
        functools.partial(back_kernel, half, tpc),
        out_shape=jax.ShapeDtypeStruct((half, tpc) + tile, f32),
        in_specs=[sm, vm, vm, vm, vm, vm],
        out_specs=vm,
        compiler_params=params,
        name="back",
    )(meta, f, cin, alpha, message, theirs)
    back = lax.all_to_all(solved, "lev", 0, 0, axis_index_groups=groups, tiled=True)
    return pl.pallas_call(
        functools.partial(join_kernel, nb, tc, tpc),
        out_shape=jax.ShapeDtypeStruct(tracer.shape, f32),
        in_specs=[vm],
        out_specs=vm,
        compiler_params=params,
        name="join",
    )(back)


def solution(mesh):
    placed = (
        P(None, "lev", "band", None),
        P("lev", "band", None),
        P("lev", "band", None),
        P("lev", "band", None),
        P("lev", "band", None),
        P(),
        P("band", None),
        P(),
        P(),
    )
    return jax.shard_map(
        shards, mesh=mesh, in_specs=placed, out_specs=P(None, "lev", "band", None), check_vma=False
    )
```

```python
import functools

import jax
import jax.numpy as jnp
from jax import lax
from jax.experimental import pallas as pl
from jax.experimental.pallas import tpu as pltpu
from jax.sharding import PartitionSpec as P

LANES = 128
ROWS = 8
EAST, NORTH, UP, DIFF, EDGE, EXTRA = 0, 1, 2, 3, 4, 5
f32 = jnp.float32
VMEM_LIMIT = 32 * 1024 * 1024


def lanes_iota():
    return lax.broadcasted_iota(jnp.int32, (ROWS, LANES), 1)


def rows_iota():
    return lax.broadcasted_iota(jnp.int32, (ROWS, LANES), 0)


def pack_kernel(
    nb, tc, tpc, meta, tracer, east, north, up, diff, kmt, out, cells, fields, depth, extra, sem
):
    loads = [
        pltpu.make_async_copy(kmt, depth, sem.at[0]),
        pltpu.make_async_copy(east, fields.at[pl.ds(EAST, 1)], sem.at[1]),
        pltpu.make_async_copy(north, fields.at[pl.ds(NORTH, 1)], sem.at[2]),
        pltpu.make_async_copy(up, fields.at[pl.ds(UP, 1)], sem.at[3]),
        pltpu.make_async_copy(diff, fields.at[pl.ds(DIFF, 1)], sem.at[4]),
    ]
    chunks = [
        pltpu.make_async_copy(
            tracer.at[pl.ds(c * tpc, tpc), 0], cells.at[pl.ds(c * tpc, tpc)], sem.at[5 + c]
        )
        for c in range(tc)
    ]
    for copy in loads + chunks:
        copy.start()
    for copy in loads:
        copy.wait()
    level = meta[0]
    lane = lanes_iota()
    cols = [slice(b * LANES, (b + 1) * LANES) for b in range(nb)]
    wet = [(level < depth[:, cols[b]]).astype(f32) for b in range(nb)]
    flow = [None]
    for b in range(1, nb):
        ends = fields[EAST, :, cols[b - 1]][:, LANES - 1 :]
        ends = ends * wet[b - 1][:, LANES - 1 :] * wet[b][:, :1]
        flow.append(jnp.broadcast_to(ends, (ROWS, LANES)))
    stores = []
    for c in range(tc):
        chunks[c].wait()
        for b in range(nb):
            r = b * tc + c
            copy = pltpu.make_async_copy(
                cells.at[pl.ds(c * tpc, tpc), :, pl.ds(b * LANES, LANES)],
                out.at[r, pl.ds(0, tpc)],
                sem.at[5 + tc + 2 * r],
            )
            copy.start()
            stores.append(copy)
        faces = [jnp.zeros((ROWS, LANES), f32) for _ in range(nb)]
        for t in range(tpc):
            for b in range(1, nb):
                west = pltpu.roll(cells[c * tpc + t, :, cols[b - 1]], (2 * t + 1) % LANES, 1)
                here = cells[c * tpc + t, :, cols[b]]
                here = pltpu.roll(here, 2 * t, 1) if t else here
                face = jnp.maximum(flow[b], 0.0) * west + jnp.minimum(flow[b], 0.0) * here
                faces[b] = jnp.where(lane == 2 * t, face, faces[b])
        for b in range(nb):
            r = b * tc + c
            edge = faces[b]
            if b + 1 < nb:
                edge = edge - pltpu.roll(faces[b + 1], LANES - 1, 1)
            for i in range(4):
                extra[r, i] = fields[i, :, cols[b]]
            extra[r, EDGE] = edge
            copy = pltpu.make_async_copy(
                extra.at[r], out.at[r, pl.ds(tpc, EXTRA)], sem.at[6 + tc + 2 * r]
            )
            copy.start()
            stores.append(copy)
    for copy in stores:
        copy.wait()


def solve_kernel(
    half, tpc, meta, thickness, group, rates, got, kmt_all, across,
    f_out, cin_out, alpha_out, message,
):
    upper, block, chunk = meta[0], meta[1], meta[2]
    sign = 1.0 - 2.0 * upper.astype(f32)
    kmt = kmt_all[:, pl.ds(pl.multiple_of(block * LANES, LANES), LANES)]
    lane, row = lanes_iota(), rows_iota()
    ends = jnp.logical_or(lane == 0, lane == LANES - 1)
    first = jnp.where(upper == 1, 2 * half - 1, 0)
    step = 1 - 2 * upper

    def level_of(o):
        return first + step * o

    def slot_of(o):
        return jnp.where(upper == 1, half - 1 - o, o)

    zero = jnp.zeros((ROWS, LANES), f32)
    cin = tout = outer = add_mid = zero
    for o in range(half):
        k = level_of(o)
        slot = slot_of(o)
        dz, dz_next = thickness[k], thickness[level_of(o + 1)]
        wet = (k < kmt).astype(f32)
        wet_next = (level_of(o + 1) < kmt).astype(f32)
        if o + 1 < half:
            face = jnp.where(upper == 1, slot, slot_of(o + 1))
            w, g = got[face, tpc + UP], got[face, tpc + DIFF]
        else:
            w = jnp.where(upper == 1, got[0, tpc + UP], across[0])
            g = jnp.where(upper == 1, got[0, tpc + DIFF], across[1])
        open_face = wet * wet_next
        w = sign * w * open_face
        g = g * open_face / (0.5 * (dz + dz_next))
        dz_min = jnp.minimum(dz, dz_next)
        pos, neg = dz_min * jnp.maximum(w, 0.0), dz_min * jnp.minimum(w, 0.0)
        inner = -g / dz
        tin = pos / dz
        mid = wet + add_mid + neg / dz
        alpha = 1.0 / (1.0 - outer - inner - outer * cin)
        cin_new = inner * alpha
        east = got[slot, tpc + EAST] * wet * pltpu.roll(wet, LANES - 1, 1)
        east = jnp.where(lane == LANES - 1, 0.0, east)
        north = got[slot, tpc + NORTH] * wet * pltpu.roll(wet, ROWS - 1, 0)
        north = jnp.where(row == ROWS - 1, 0.0, north)
        e_pos, e_neg = jnp.maximum(east, 0.0), jnp.minimum(east, 0.0)
        n_pos, n_neg = jnp.maximum(north, 0.0), jnp.minimum(north, 0.0)
        mid = mid - e_pos - n_pos + pltpu.roll(e_neg, 1, 1) + pltpu.roll(n_neg, 1, 0)
        e_pos, n_pos = pltpu.roll(e_pos, 1, 1), pltpu.roll(n_pos, 1, 0)
        edges = got[slot, tpc + EDGE]
        last = o + 1 == half
        prev_slot = slot_of(o - 1) if o else None
        next_slot = None if last else slot_of(o + 1)
        tout_next = -neg / dz_next
        outer_next = -g / dz_next
        for t in range(tpc):
            c = got[slot, t]
            rate = rates[group[chunk * tpc + t], k]
            star = c * (mid - rate * wet)
            if o:
                star += tout * got[prev_slot, t]
            if not last:
                star += tin * got[next_slot, t]
            star += e_pos * pltpu.roll(c, 1, 1) - e_neg * pltpu.roll(c, LANES - 1, 1)
            star += n_pos * pltpu.roll(c, 1, 0) - n_neg * pltpu.roll(c, ROWS - 1, 0)
            edge = pltpu.roll(edges, LANES - 2 * t, 1) if t else edges
            star += jnp.where(ends, edge, 0.0)
            if o:
                star -= outer * f_out[o - 1, t]
            f = alpha * star
            f_out[o, t] = f
            if last:
                message[t] = tout_next * c - outer_next * f
        cin_out[o] = cin_new
        if last:
            alpha_out[0] = alpha
            alpha_out[1] = outer_next
            message[tpc] = alpha
        cin, tout, outer, add_mid = cin_new, tout_next, outer_next, -pos / dz_next


def back_kernel(half, tpc, meta, f_in, cin, alpha, sent, got, out):
    upper = meta[0]
    slots = [jnp.where(upper == 1, half - 1 - o, o) for o in range(half)]
    other = cin[half - 1] * got[tpc]
    scale = 1.0 / (1.0 - other * alpha[1])
    mine, theirs = scale * alpha[0], scale * other
    for t in range(tpc):
        x = f_in[half - 1, t] + (mine * got[t] - theirs * sent[t])
        out[slots[half - 1], t] = x
        for o in range(half - 2, -1, -1):
            x = f_in[o, t] - cin[o] * x
            out[slots[o], t] = x


def join_kernel(nb, tc, tpc, got, out, sem):
    copies = []
    for b in range(nb):
        for c in range(tc):
            r = b * tc + c
            copies.append(
                pltpu.make_async_copy(
                    got.at[r],
                    out.at[pl.ds(c * tpc, tpc), 0, :, pl.ds(b * LANES, LANES)],
                    sem.at[r],
                )
            )
    for copy in copies:
        copy.start()
    for copy in copies:
        copy.wait()


def shards(tracer, east_flow, north_flow, up_flow, diffusivity, thickness, kmt, group, group_rate):
    ntr, ldev, ny, nx = tracer.shape
    count = lax.axis_size("lev")
    half = count // 2
    nb = nx // LANES
    tc = half // nb
    tpc = ntr // tc
    assert ldev == 1 and ny == ROWS and nb * LANES == nx and tc * nb == half and tpc * tc == ntr
    index = lax.axis_index("lev").astype(jnp.int32)
    upper, rank = index // half, index % half
    meta = jnp.stack([upper, rank // tc, rank % tc, index])
    vm = pl.BlockSpec(memory_space=pltpu.VMEM)
    sm = pl.BlockSpec(memory_space=pltpu.SMEM)
    hbm = pl.BlockSpec(memory_space=pltpu.HBM)
    params = pltpu.CompilerParams(vmem_limit_bytes=VMEM_LIMIT)
    groups = [[h * half + i for i in range(half)] for h in range(2)]

    pieces = pl.pallas_call(
        functools.partial(pack_kernel, nb, tc, tpc),
        out_shape=jax.ShapeDtypeStruct((half, tpc + EXTRA, ROWS, LANES), f32),
        in_specs=[sm] + [hbm] * 6,
        out_specs=hbm,
        scratch_shapes=[
            pltpu.VMEM((ntr, ny, nx), f32),
            pltpu.VMEM((4, ny, nx), f32),
            pltpu.VMEM((ny, nx), jnp.int32),
            pltpu.VMEM((half, EXTRA, ROWS, LANES), f32),
            pltpu.SemaphoreType.DMA((5 + tc + 2 * half,)),
        ],
        compiler_params=params,
        name="pack",
    )(index[None], tracer, east_flow, north_flow, up_flow, diffusivity, kmt)
    got = lax.all_to_all(pieces, "lev", 0, 0, axis_index_groups=groups, tiled=True)

    fields = jnp.concatenate([up_flow, diffusivity], 0)
    across = jnp.zeros((2, ROWS, LANES), f32)
    for r in range(half):
        cols = lax.slice_in_dim(fields, (r // tc) * LANES, (r // tc + 1) * LANES, axis=2)
        across = across + lax.ppermute(cols, "lev", [(half, r)])

    tile = (ROWS, LANES)
    f, cin, alpha, message = pl.pallas_call(
        functools.partial(solve_kernel, half, tpc),
        out_shape=(
            jax.ShapeDtypeStruct((half, tpc) + tile, f32),
            jax.ShapeDtypeStruct((half,) + tile, f32),
            jax.ShapeDtypeStruct((2,) + tile, f32),
            jax.ShapeDtypeStruct((tpc + 1,) + tile, f32),
        ),
        in_specs=[sm, sm, sm, sm, vm, vm, vm],
        out_specs=(vm, vm, vm, vm),
        compiler_params=params,
        name="solve",
    )(meta, thickness, group, group_rate, got, kmt, across)
    theirs = lax.ppermute(
        message, "lev", [(i, (i + half) % count) for i in range(count)]
    )
    solved = pl.pallas_call(
        functools.partial(back_kernel, half, tpc),
        out_shape=jax.ShapeDtypeStruct((half, tpc) + tile, f32),
        in_specs=[sm, vm, vm, vm, vm, vm],
        out_specs=vm,
        compiler_params=params,
        name="back",
    )(meta, f, cin, alpha, message, theirs)
    back = lax.all_to_all(solved, "lev", 0, 0, axis_index_groups=groups, tiled=True)
    return pl.pallas_call(
        functools.partial(join_kernel, nb, tc, tpc),
        out_shape=jax.ShapeDtypeStruct(tracer.shape, f32),
        in_specs=[vm],
        out_specs=hbm,
        scratch_shapes=[pltpu.SemaphoreType.DMA((half,))],
        compiler_params=params,
        name="join",
    )(back)


def solution(mesh):
    placed = (
        P(None, "lev", "band", None),
        P("lev", "band", None),
        P("lev", "band", None),
        P("lev", "band", None),
        P("lev", "band", None),
        P(),
        P("band", None),
        P(),
        P(),
    )
    return jax.shard_map(
        shards, mesh=mesh, in_specs=placed, out_specs=P(None, "lev", "band", None), check_vma=False
    )
```

```python
import functools

import jax
import jax.numpy as jnp
from jax import lax
from jax.experimental import pallas as pl
from jax.experimental.pallas import tpu as pltpu
from jax.sharding import PartitionSpec as P

LANES = 128
ROWS = 8
EAST, NORTH, UP, DIFF, EDGE, EXTRA = 0, 1, 2, 3, 4, 5
f32 = jnp.float32
VMEM_LIMIT = 16 * 1024 * 1024
PACK_LIMIT = 60 * 1024 * 1024


def lanes_iota():
    return lax.broadcasted_iota(jnp.int32, (ROWS, LANES), 1)


def rows_iota():
    return lax.broadcasted_iota(jnp.int32, (ROWS, LANES), 0)


def start_order(half):
    far, near = half // 2, half // 4
    kind = lambda d: -((d & far) > 0) - ((d & near) > 0)
    return sorted(range(1, half), key=lambda d: (d < 2, kind(d), d & 1, -d)) + [0]


def place(index, nb, tc):
    half = nb * tc
    rank = lax.rem(index, half)
    return lax.div(index, half), rank, lax.div(rank, tc), lax.rem(rank, tc)


def pack_kernel(nb, tc, tpc, index, tracer, east, north, up, diff, kmt, *refs):
    half = nb * tc
    out, (cells, fields, depth, extra, sem) = refs[:half], refs[half:]
    _, rank, _, _ = place(index[0], nb, tc)
    loads = [
        pltpu.make_async_copy(kmt, depth, sem.at[0]),
        pltpu.make_async_copy(east, fields.at[pl.ds(EAST, 1)], sem.at[1]),
        pltpu.make_async_copy(north, fields.at[pl.ds(NORTH, 1)], sem.at[2]),
        pltpu.make_async_copy(up, fields.at[pl.ds(UP, 1)], sem.at[3]),
        pltpu.make_async_copy(diff, fields.at[pl.ds(DIFF, 1)], sem.at[4]),
    ]
    chunks = [
        pltpu.make_async_copy(
            tracer.at[pl.ds(c * tpc, tpc), 0], cells.at[pl.ds(c * tpc, tpc)], sem.at[5 + c]
        )
        for c in range(tc)
    ]
    for copy in chunks + loads:
        copy.start()
    for copy in chunks:
        copy.wait()
    stores = []
    for i, d in enumerate(start_order(half)):
        r = rank ^ d
        cut = pl.ds(pl.multiple_of(lax.div(r, tc) * LANES, LANES), LANES)
        copy = pltpu.make_async_copy(
            cells.at[pl.ds(lax.rem(r, tc) * tpc, tpc), :, cut],
            out[d].at[pl.ds(0, tpc)],
            sem.at[5 + tc + i],
        )
        copy.start()
        stores.append(copy)
    for copy in loads:
        copy.wait()
    lane = lanes_iota()
    cols = [slice(b * LANES, (b + 1) * LANES) for b in range(nb)]
    wet = [(index[0] < depth[:, cols[b]]).astype(f32) for b in range(nb)]
    flow = [None]
    for b in range(1, nb):
        ends = fields[EAST, :, cols[b - 1]][:, LANES - 1 :]
        ends = ends * wet[b - 1][:, LANES - 1 :] * wet[b][:, :1]
        flow.append(jnp.broadcast_to(ends, (ROWS, LANES)))
    for c in range(tc):
        faces = [jnp.zeros((ROWS, LANES), f32) for _ in range(nb)]
        for t in range(tpc):
            for b in range(1, nb):
                west = pltpu.roll(cells[c * tpc + t, :, cols[b - 1]], (2 * t + 1) % LANES, 1)
                here = cells[c * tpc + t, :, cols[b]]
                here = pltpu.roll(here, 2 * t, 1) if t else here
                face = jnp.maximum(flow[b], 0.0) * west + jnp.minimum(flow[b], 0.0) * here
                faces[b] = jnp.where(lane == 2 * t, face, faces[b])
        for b in range(nb):
            edge = faces[b]
            if b + 1 < nb:
                edge = edge - pltpu.roll(faces[b + 1], LANES - 1, 1)
            for i in range(4):
                extra[b * tc + c, i] = fields[i, :, cols[b]]
            extra[b * tc + c, EDGE] = edge
    for d in range(half):
        copy = pltpu.make_async_copy(
            extra.at[rank ^ d], out[d].at[pl.ds(tpc, EXTRA)], sem.at[5 + tc + half + d]
        )
        copy.start()
        stores.append(copy)
    for copy in stores:
        copy.wait()


def keep_kernel(piece, own, sem):
    copy = pltpu.make_async_copy(piece, own, sem.at[0])
    copy.start()
    copy.wait()


def pick_kernel(nb, tc, tpc, index, *refs):
    arrived, out = refs[:-1], refs[-1]
    _, rank, _, _ = place(index[0], nb, tc)
    for i in range(2):
        field = arrived[0][tpc + UP + i]
        for d, piece in zip(start_order(nb * tc)[1:], arrived[1:]):
            field = jnp.where(rank == d, piece[tpc + UP + i], field)
        out[i] = field


def solve_kernel(nb, tc, tpc, index, thickness, group, rates, kmt_all, *refs):
    half = nb * tc
    arrived, (f_out, cin_out, base_out, cells_out, got) = refs[:half], refs[half:]
    upper, rank, block, chunk = place(index[0], nb, tc)
    for d, piece in zip(start_order(half), arrived):
        for t in range(tpc + EXTRA):
            got[rank ^ d, t] = piece[t]
    sign = 1.0 - 2.0 * upper.astype(f32)
    kmt = kmt_all[:, pl.ds(pl.multiple_of(block * LANES, LANES), LANES)]
    lane, row = lanes_iota(), rows_iota()
    ends = jnp.logical_or(lane == 0, lane == LANES - 1)
    first = jnp.where(upper == 1, 2 * half - 1, 0)
    step = 1 - 2 * upper

    def level_of(o):
        return first + step * o

    def slot_of(o):
        return jnp.where(upper == 1, half - 1 - o, o)

    zero = jnp.zeros((ROWS, LANES), f32)
    cin = tout = outer = add_mid = zero
    for o in range(half):
        k = level_of(o)
        slot = slot_of(o)
        dz, dz_next = thickness[k], thickness[level_of(o + 1)]
        wet = (k < kmt).astype(f32)
        wet_next = (level_of(o + 1) < kmt).astype(f32)
        last = o + 1 == half
        mid = wet + add_mid
        denom = 1.0 - outer - outer * cin
        if not last:
            face = jnp.where(upper == 1, slot, slot_of(o + 1))
            pos, neg, g = interface(
                got[face, tpc + UP], got[face, tpc + DIFF], sign, wet * wet_next, dz, dz_next
            )
            mid = mid + neg / dz
            tin = pos / dz
            inner = -g / dz
            alpha = 1.0 / (denom - inner)
        east = got[slot, tpc + EAST] * wet * pltpu.roll(wet, LANES - 1, 1)
        east = jnp.where(lane == LANES - 1, 0.0, east)
        north = got[slot, tpc + NORTH] * wet * pltpu.roll(wet, ROWS - 1, 0)
        north = jnp.where(row == ROWS - 1, 0.0, north)
        e_pos, e_neg = jnp.maximum(east, 0.0), jnp.minimum(east, 0.0)
        n_pos, n_neg = jnp.maximum(north, 0.0), jnp.minimum(north, 0.0)
        mid = mid - e_pos - n_pos + pltpu.roll(e_neg, 1, 1) + pltpu.roll(n_neg, 1, 0)
        e_pos, n_pos = pltpu.roll(e_pos, 1, 1), pltpu.roll(n_pos, 1, 0)
        edges = got[slot, tpc + EDGE]
        prev_slot = slot_of(o - 1) if o else None
        next_slot = None if last else slot_of(o + 1)
        for t in range(tpc):
            c = got[slot, t]
            rate = rates[group[chunk * tpc + t], k]
            star = c * (mid - rate * wet)
            if o:
                star += tout * got[prev_slot, t]
            if not last:
                star += tin * got[next_slot, t]
            star += e_pos * pltpu.roll(c, 1, 1) - e_neg * pltpu.roll(c, LANES - 1, 1)
            star += n_pos * pltpu.roll(c, 1, 0) - n_neg * pltpu.roll(c, ROWS - 1, 0)
            edge = pltpu.roll(edges, LANES - 2 * t, 1) if t else edges
            star += jnp.where(ends, edge, 0.0)
            if o:
                star -= outer * f_out[o - 1, t]
            f_out[o, t] = star if last else alpha * star
            if last:
                cells_out[t] = c
        if last:
            base_out[0] = denom
            base_out[1] = wet * wet_next
        else:
            cin = inner * alpha
            cin_out[o] = cin
            tout, outer, add_mid = -neg / dz_next, -g / dz_next, -pos / dz_next


def interface(w, g, sign, open_face, dz, dz_next):
    w = sign * w * open_face
    dz_min = jnp.minimum(dz, dz_next)
    g = g * open_face / (0.5 * (dz + dz_next))
    return dz_min * jnp.maximum(w, 0.0), dz_min * jnp.minimum(w, 0.0), g


def seam_kernel(nb, tc, tpc, index, thickness, star, cells, base, own, other, f_out, coef_out, message):
    half = nb * tc
    upper, _, _, _ = place(index[0], nb, tc)
    sign = 1.0 - 2.0 * upper.astype(f32)
    dz = thickness[half - 1 + upper]
    dz_next = thickness[half - upper]
    w = jnp.where(upper == 1, own[0], other[0])
    g = jnp.where(upper == 1, own[1], other[1])
    pos, neg, g = interface(w, g, sign, base[1], dz, dz_next)
    inner, outer_next = -g / dz, -g / dz_next
    mid, tout_next = neg / dz, -neg / dz_next
    alpha = 1.0 / (base[0] - inner)
    for t in range(tpc):
        c = cells[t]
        f = alpha * (star[half - 1, t] + mid * c)
        f_out[t] = f
        message[t] = tout_next * c - outer_next * f
    coef_out[0] = inner * alpha
    coef_out[1] = alpha
    coef_out[2] = outer_next
    message[tpc] = alpha


def back_kernel(nb, tc, tpc, index, f_in, cin, f_last, coef, sent, got, *refs):
    half = nb * tc
    out, (solved,) = refs[:half], refs[half:]
    upper, rank, _, _ = place(index[0], nb, tc)
    slots = [jnp.where(upper == 1, half - 1 - o, o) for o in range(half)]
    other = coef[0] * got[tpc]
    scale = 1.0 / (1.0 - other * coef[2])
    mine, theirs = scale * coef[1], scale * other
    for t in range(tpc):
        x = f_last[t] + (mine * got[t] - theirs * sent[t])
        solved[slots[half - 1], t] = x
        for o in range(half - 2, -1, -1):
            x = f_in[o, t] - cin[o] * x
            solved[slots[o], t] = x
    for d in range(half):
        for t in range(tpc):
            out[d][t] = solved[rank ^ d, t]


def join_kernel(nb, tc, tpc, index, *refs):
    arrived, out, sem = refs[:-2], refs[-2], refs[-1]
    copies = []
    _, rank, _, _ = place(index[0], nb, tc)
    for d, piece in zip(start_order(len(arrived)), arrived):
        r = rank ^ d
        cols = pl.ds(pl.multiple_of(lax.div(r, tc) * LANES, LANES), LANES)
        copies.append(
            pltpu.make_async_copy(
                piece, out.at[pl.ds(lax.rem(r, tc) * tpc, tpc), 0, :, cols], sem.at[d]
            )
        )
    for copy in copies:
        copy.start()
    for copy in copies:
        copy.wait()


def shards(tracer, east_flow, north_flow, up_flow, diffusivity, thickness, kmt, group, group_rate):
    ntr, ldev, ny, nx = tracer.shape
    count = lax.axis_size("lev")
    half = count // 2
    nb = nx // LANES
    tc = half // nb
    tpc = ntr // tc
    assert ldev == 1 and ny == ROWS and nb * LANES == nx and tc * nb == half and tpc * tc == ntr
    index = lax.axis_index("lev").astype(jnp.int32)[None]
    tile = (ROWS, LANES)
    vm = pl.BlockSpec(memory_space=pltpu.VMEM)
    sm = pl.BlockSpec(memory_space=pltpu.SMEM)
    hbm = pl.BlockSpec(memory_space=pltpu.HBM)
    anywhere = pl.BlockSpec(memory_space=pl.ANY)
    params = pltpu.CompilerParams(vmem_limit_bytes=VMEM_LIMIT)

    def flip(value, bits):
        return lax.ppermute(value, "lev", [(i, i ^ bits) for i in range(count)])

    pieces = pl.pallas_call(
        functools.partial(pack_kernel, nb, tc, tpc),
        out_shape=(jax.ShapeDtypeStruct((tpc + EXTRA,) + tile, f32),) * half,
        in_specs=[sm] + [hbm] * 6,
        out_specs=(hbm,) * half,
        scratch_shapes=[
            pltpu.VMEM((ntr, ny, nx), f32),
            pltpu.VMEM((4, ny, nx), f32),
            pltpu.VMEM((ny, nx), jnp.int32),
            pltpu.VMEM((half, EXTRA) + tile, f32),
            pltpu.SemaphoreType.DMA((5 + tc + 2 * half,)),
        ],
        compiler_params=pltpu.CompilerParams(vmem_limit_bytes=PACK_LIMIT),
        name="pack",
    )(index, tracer, east_flow, north_flow, up_flow, diffusivity, kmt)
    order = start_order(half)

    def exchange(values):
        return [flip(values[d], d) if d else values[d] for d in order]

    arrived = exchange(pieces)
    arrived[-1] = pl.pallas_call(
        keep_kernel,
        out_shape=jax.ShapeDtypeStruct((tpc + EXTRA,) + tile, f32),
        in_specs=[anywhere],
        out_specs=vm,
        scratch_shapes=[pltpu.SemaphoreType.DMA((1,))],
        compiler_params=params,
        name="keep",
    )(arrived[-1])
    own = pl.pallas_call(
        functools.partial(pick_kernel, nb, tc, tpc),
        out_shape=jax.ShapeDtypeStruct((2,) + tile, f32),
        in_specs=[sm] + [vm] * half,
        out_specs=vm,
        compiler_params=params,
        name="pick",
    )(index, *arrived)
    other = flip(own, half)
    f, cin, base, cells = pl.pallas_call(
        functools.partial(solve_kernel, nb, tc, tpc),
        out_shape=(
            jax.ShapeDtypeStruct((half, tpc) + tile, f32),
            jax.ShapeDtypeStruct((half - 1,) + tile, f32),
            jax.ShapeDtypeStruct((2,) + tile, f32),
            jax.ShapeDtypeStruct((tpc,) + tile, f32),
        ),
        in_specs=[sm, sm, sm, sm, vm] + [vm] * half,
        out_specs=(vm, vm, vm, vm),
        scratch_shapes=[pltpu.VMEM((half, tpc + EXTRA) + tile, f32)],
        compiler_params=params,
        name="solve",
    )(index, thickness, group, group_rate, kmt, *arrived)
    f_last, coef, message = pl.pallas_call(
        functools.partial(seam_kernel, nb, tc, tpc),
        out_shape=(
            jax.ShapeDtypeStruct((tpc,) + tile, f32),
            jax.ShapeDtypeStruct((3,) + tile, f32),
            jax.ShapeDtypeStruct((tpc + 1,) + tile, f32),
        ),
        in_specs=[sm, sm, vm, vm, vm, vm, vm],
        out_specs=(vm, vm, vm),
        compiler_params=params,
        name="seam",
    )(index, thickness, f, cells, base, own, other)
    theirs = flip(message, half)
    solved = pl.pallas_call(
        functools.partial(back_kernel, nb, tc, tpc),
        out_shape=(jax.ShapeDtypeStruct((tpc,) + tile, f32),) * half,
        in_specs=[sm, vm, vm, vm, vm, vm, vm],
        out_specs=(vm,) * half,
        scratch_shapes=[pltpu.VMEM((half, tpc) + tile, f32)],
        compiler_params=params,
        name="back",
    )(index, f, cin, f_last, coef, message, theirs)
    back = exchange(solved)
    return pl.pallas_call(
        functools.partial(join_kernel, nb, tc, tpc),
        out_shape=jax.ShapeDtypeStruct(tracer.shape, f32),
        in_specs=[sm] + [anywhere] * half,
        out_specs=hbm,
        scratch_shapes=[pltpu.SemaphoreType.DMA((half,))],
        compiler_params=params,
        name="join",
    )(index, *back)


def solution(mesh):
    placed = (
        P(None, "lev", "band", None),
        P("lev", "band", None),
        P("lev", "band", None),
        P("lev", "band", None),
        P("lev", "band", None),
        P(),
        P("band", None),
        P(),
        P(),
    )
    return jax.shard_map(
        shards, mesh=mesh, in_specs=placed, out_specs=P(None, "lev", "band", None), check_vma=False
    )
```

```python
import functools

import jax
import jax.numpy as jnp
from jax import lax
from jax.experimental import pallas as pl
from jax.experimental.pallas import tpu as pltpu
from jax.sharding import PartitionSpec as P

LANES = 128
ROWS = 8
THERE, HOME = "none", "none"
WAIT = 1
EAST, NORTH, UP, DIFF, EDGE, EXTRA = 0, 1, 2, 3, 4, 5
f32 = jnp.float32
VMEM_LIMIT = 16 * 1024 * 1024
PACK_LIMIT = 60 * 1024 * 1024


def lanes_iota():
    return lax.broadcasted_iota(jnp.int32, (ROWS, LANES), 1)


def rows_iota():
    return lax.broadcasted_iota(jnp.int32, (ROWS, LANES), 0)


def devices(half):
    far, near = half // 2, half // 4
    crossed = lambda d: ((d & far) > 0) + ((d & near) > 0)
    return sorted(range(1, half), key=lambda d: (d < 2, d & 1, -crossed(d), -d)) + [0]


def pairing(half, which):
    if which == "none":
        return ()
    far = half // 2 | half // 4
    return tuple(d for d in range(2, half, 2) if which == "all" or d & far == far)


def sends(half, paired):
    order = [(d, d in paired) for d in devices(half) if d > 1 and (d % 2 == 0 or d - 1 not in paired)]
    return order + [(0, True)] if paired else order + [(1, False), (0, False)]


def by_level(half, paired, refs, rank):
    order = sends(half, paired)
    direct = [(rank ^ d, refs[j].at[0] if both else refs[j]) for j, (d, both) in enumerate(order)]
    swapped = [d ^ 1 for d, both in order if both]
    return direct + [(rank ^ d, refs[len(order)].at[j]) for j, d in enumerate(swapped)]


def n_arrived(half, paired):
    return len(sends(half, paired)) + (1 if paired else 0)


def place(nb, tc):
    half = nb * tc
    index = lax.axis_index("lev")
    rank = lax.rem(index, half)
    return lax.div(index, half), rank, lax.div(rank, tc), lax.rem(rank, tc)


def pack_kernel(nb, tc, tpc, paired, tracer, east, north, up, diff, kmt, *refs):
    half = nb * tc
    _, rank, _, _ = place(nb, tc)
    order = sends(half, paired)
    out = {}
    for j, (d, both) in enumerate(order):
        if both:
            out[d], out[d ^ 1] = refs[j].at[0], refs[j].at[1]
        else:
            out[d] = refs[j]
    cells, fields, depth, extra, sem, store_sem = refs[len(order) :]
    loads = [
        pltpu.make_async_copy(kmt, depth, sem.at[0]),
        pltpu.make_async_copy(east, fields.at[pl.ds(EAST, 1)], sem.at[1]),
        pltpu.make_async_copy(north, fields.at[pl.ds(NORTH, 1)], sem.at[2]),
        pltpu.make_async_copy(up, fields.at[pl.ds(UP, 1)], sem.at[3]),
        pltpu.make_async_copy(diff, fields.at[pl.ds(DIFF, 1)], sem.at[4]),
    ]
    chunks = [
        pltpu.make_async_copy(
            tracer.at[pl.ds(c * tpc, tpc), 0], cells.at[pl.ds(c * tpc, tpc)], sem.at[5 + c]
        )
        for c in range(tc)
    ]
    for copy in chunks + loads:
        copy.start()
    for copy in chunks:
        copy.wait()
    stores = []
    for d in devices(half):
        r = rank ^ d
        cut = pl.ds(pl.multiple_of(lax.div(r, tc) * LANES, LANES), LANES)
        copy = pltpu.make_async_copy(
            cells.at[pl.ds(lax.rem(r, tc) * tpc, tpc), :, cut], out[d].at[pl.ds(0, tpc)], store_sem.at[0, d]
        )
        copy.start()
        stores.append(copy)
    for copy in loads:
        copy.wait()
    lane = lanes_iota()
    cols = [slice(b * LANES, (b + 1) * LANES) for b in range(nb)]
    wet = [(lax.axis_index("lev") < depth[:, cols[b]]).astype(f32) for b in range(nb)]
    flow = [None]
    for b in range(1, nb):
        ends = fields[EAST, :, cols[b - 1]][:, LANES - 1 :]
        ends = ends * wet[b - 1][:, LANES - 1 :] * wet[b][:, :1]
        flow.append(jnp.broadcast_to(ends, (ROWS, LANES)))
    for c in range(tc):
        faces = [jnp.zeros((ROWS, LANES), f32) for _ in range(nb)]
        for t in range(tpc):
            for b in range(1, nb):
                west = pltpu.roll(cells[c * tpc + t, :, cols[b - 1]], (2 * t + 1) % LANES, 1)
                here = cells[c * tpc + t, :, cols[b]]
                here = pltpu.roll(here, 2 * t, 1) if t else here
                face = jnp.maximum(flow[b], 0.0) * west + jnp.minimum(flow[b], 0.0) * here
                faces[b] = jnp.where(lane == 2 * t, face, faces[b])
        for b in range(nb):
            edge = faces[b]
            if b + 1 < nb:
                edge = edge - pltpu.roll(faces[b + 1], LANES - 1, 1)
            for i in range(4):
                extra[b * tc + c, i] = fields[i, :, cols[b]]
            extra[b * tc + c, EDGE] = edge
    for d in devices(half):
        copy = pltpu.make_async_copy(
            extra.at[rank ^ d], out[d].at[pl.ds(tpc, EXTRA)], store_sem.at[1, d]
        )
        copy.start()
        stores.append(copy)
    for copy in stores:
        copy.wait()


def keep_kernel(prepared, piece, own, sem):
    del prepared
    copy = pltpu.make_async_copy(piece, own, sem.at[0])
    copy.start()
    copy.wait()


def relay_kernel(nb, tc, tpc, up, diff, *refs):
    half = nb * tc
    arrived, out = refs[:-1], refs[-1]
    _, rank, block, _ = place(nb, tc)
    cols = pl.ds(pl.multiple_of(block * LANES, LANES), LANES)
    for i, level in enumerate((up, diff)):
        field = level[0, :, cols]
        for d, even in zip(devices(half), arrived):
            field = jnp.where(rank == d, even[tpc + UP + i], field)
        out[i] = field


def pick_kernel(nb, tc, relayed, arrived, own):
    _, rank, _, _ = place(nb, tc)
    for i in range(2):
        own[i] = jnp.where(lax.rem(rank, 2) == 1, arrived[i], relayed[i])


def prep_kernel(nb, tc, tpc, thickness, group, rates, kmt_all, wet, depth, decay):
    half = nb * tc
    upper, _, block, chunk = place(nb, tc)
    kmt = kmt_all[:, pl.ds(pl.multiple_of(block * LANES, LANES), LANES)]
    for o in range(half + 1):
        k = jnp.where(upper == 1, 2 * half - 1 - o, o)
        wet[o] = (k < kmt).astype(f32)
        depth[o] = jnp.full((ROWS, LANES), thickness[k], f32)
        if o < half:
            for t in range(tpc):
                decay[o, pl.ds(t, 1)] = jnp.full((1, LANES), rates[group[chunk * tpc + t], k], f32)


def solve_kernel(nb, tc, tpc, paired, wets, depths, decay, *refs):
    half = nb * tc
    arrived = refs[: n_arrived(half, paired)]
    f_out, cells_out, cin_out, base_out, got = refs[-5:]
    upper, rank, _, _ = place(nb, tc)
    for slot, piece in by_level(half, paired, arrived, rank):
        for t in range(tpc + EXTRA):
            got[slot, t] = piece[t]
    sign = 1.0 - 2.0 * upper.astype(f32)
    lane, row = lanes_iota(), rows_iota()
    ends = jnp.logical_or(lane == 0, lane == LANES - 1)

    def slot_of(o):
        return jnp.where(upper == 1, half - 1 - o, o)

    zero = jnp.zeros((ROWS, LANES), f32)
    cin = tout = outer = add_mid = zero
    for o in range(half):
        slot = slot_of(o)
        dz, dz_next = depths[o], depths[o + 1]
        wet, wet_next = wets[o], wets[o + 1]
        last = o + 1 == half
        mid = wet + add_mid
        denom = 1.0 - outer - outer * cin
        if not last:
            face = jnp.where(upper == 1, slot, slot_of(o + 1))
            pos, neg, g = interface(
                got[face, tpc + UP], got[face, tpc + DIFF], sign, wet * wet_next, dz, dz_next
            )
            mid = mid + neg / dz
            tin = pos / dz
            inner = -g / dz
            alpha = 1.0 / (denom - inner)
        east = got[slot, tpc + EAST] * wet * pltpu.roll(wet, LANES - 1, 1)
        east = jnp.where(lane == LANES - 1, 0.0, east)
        north = got[slot, tpc + NORTH] * wet * pltpu.roll(wet, ROWS - 1, 0)
        north = jnp.where(row == ROWS - 1, 0.0, north)
        e_pos, e_neg = jnp.maximum(east, 0.0), jnp.minimum(east, 0.0)
        n_pos, n_neg = jnp.maximum(north, 0.0), jnp.minimum(north, 0.0)
        mid = mid - e_pos - n_pos + pltpu.roll(e_neg, 1, 1) + pltpu.roll(n_neg, 1, 0)
        e_pos, n_pos = pltpu.roll(e_pos, 1, 1), pltpu.roll(n_pos, 1, 0)
        edges = got[slot, tpc + EDGE]
        prev_slot = slot_of(o - 1) if o else None
        next_slot = None if last else slot_of(o + 1)
        for t in range(tpc):
            c = got[slot, t]
            star = c * (mid - decay[o, pl.ds(t, 1)] * wet)
            if o:
                star += tout * got[prev_slot, t]
            if not last:
                star += tin * got[next_slot, t]
            star += e_pos * pltpu.roll(c, 1, 1) - e_neg * pltpu.roll(c, LANES - 1, 1)
            star += n_pos * pltpu.roll(c, 1, 0) - n_neg * pltpu.roll(c, ROWS - 1, 0)
            edge = pltpu.roll(edges, LANES - 2 * t, 1) if t else edges
            star += jnp.where(ends, edge, 0.0)
            if o:
                star -= outer * f_out[o - 1, t]
            f_out[o, t] = star if last else alpha * star
            if last:
                cells_out[t] = c
        if last:
            base_out[0] = denom
            base_out[1] = wet * wet_next
            base_out[2] = jnp.full((ROWS, LANES), sign, f32)
            base_out[3] = dz
            base_out[4] = dz_next
        else:
            cin = inner * alpha
            cin_out[o] = cin
            tout, outer, add_mid = -neg / dz_next, -g / dz_next, -pos / dz_next


def interface(w, g, sign, open_face, dz, dz_next):
    w = sign * w * open_face
    dz_min = jnp.minimum(dz, dz_next)
    g = g * open_face / (0.5 * (dz + dz_next))
    return dz_min * jnp.maximum(w, 0.0), dz_min * jnp.minimum(w, 0.0), g


def seam_kernel(half, count, star, cells, base, own, other, f_out, coef_out, message):
    sign, dz, dz_next = base[2], base[3], base[4]
    w = jnp.where(sign < 0.0, own[0], other[0])
    g = jnp.where(sign < 0.0, own[1], other[1])
    pos, neg, g = interface(w, g, sign, base[1], dz, dz_next)
    inner, outer_next = -g / dz, -g / dz_next
    mid, tout_next = neg / dz, -neg / dz_next
    alpha = 1.0 / (base[0] - inner)
    for t in range(count):
        c = cells[t]
        f = alpha * (star[half - 1, t] + mid * c)
        f_out[t] = f
        message[t] = tout_next * c - outer_next * f
    coef_out[0] = inner * alpha
    coef_out[1] = alpha
    coef_out[2] = outer_next
    message[count] = alpha


def back_kernel(nb, tc, tpc, paired, f_in, cin, f_last, coef, sent, got, *refs):
    half = nb * tc
    out, solved = refs[:-1], refs[-1]
    upper, rank, _, _ = place(nb, tc)
    slots = [jnp.where(upper == 1, half - 1 - o, o) for o in range(half)]
    other = coef[0] * got[tpc]
    scale = 1.0 / (1.0 - other * coef[2])
    mine, theirs = scale * coef[1], scale * other
    for t in range(tpc):
        x = f_last[t] + (mine * got[t] - theirs * sent[t])
        solved[slots[half - 1], t] = x
        for o in range(half - 2, -1, -1):
            x = f_in[o, t] - cin[o] * x
            solved[slots[o], t] = x
    for (d, both), piece in zip(sends(half, paired), out):
        for t in range(tpc):
            if both:
                piece[0, t] = solved[rank ^ d, t]
                piece[1, t] = solved[rank ^ d ^ 1, t]
            else:
                piece[t] = solved[rank ^ d, t]


def join_kernel(nb, tc, tpc, paired, *refs):
    half = nb * tc
    arrived, out, sem = refs[:-2], refs[-2], refs[-1]
    copies = []
    _, rank, _, _ = place(nb, tc)
    for i, (r, piece) in enumerate(by_level(half, paired, arrived, rank)):
        cols = pl.ds(pl.multiple_of(lax.div(r, tc) * LANES, LANES), LANES)
        copies.append(
            pltpu.make_async_copy(
                piece, out.at[pl.ds(lax.rem(r, tc) * tpc, tpc), 0, :, cols], sem.at[i]
            )
        )
    for copy in copies:
        copy.start()
    for copy in copies:
        copy.wait()


def shards(tracer, east_flow, north_flow, up_flow, diffusivity, thickness, kmt, group, group_rate):
    ntr, ldev, ny, nx = tracer.shape
    count = lax.axis_size("lev")
    half = count // 2
    nb = nx // LANES
    tc = half // nb
    tpc = ntr // tc
    assert ldev == 1 and ny == ROWS and nb * LANES == nx and tc * nb == half and tpc * tc == ntr
    tile = (ROWS, LANES)
    vm = pl.BlockSpec(memory_space=pltpu.VMEM)
    sm = pl.BlockSpec(memory_space=pltpu.SMEM)
    hbm = pl.BlockSpec(memory_space=pltpu.HBM)
    anywhere = pl.BlockSpec(memory_space=pl.ANY)
    params = pltpu.CompilerParams(vmem_limit_bytes=VMEM_LIMIT)

    def flip(value, bits):
        return lax.ppermute(value, "lev", [(i, i ^ bits) for i in range(count)])

    def struct(*shape):
        return jax.ShapeDtypeStruct(shape + tile, f32)

    def outgoing(paired, n):
        return tuple(struct(2, n) if both else struct(n) for _, both in sends(half, paired))

    def exchange(values, paired):
        order = sends(half, paired)
        moved = [flip(piece, d) if d else piece for (d, _), piece in zip(order, values)]
        if not paired:
            return moved
        other = [piece for (_, both), piece in zip(order, moved) if both]
        after = [piece for (_, both), piece in zip(order, moved) if not both][:WAIT]
        grouped = pl.pallas_call(
            regroup_kernel,
            out_shape=jax.ShapeDtypeStruct((len(other),) + other[0].shape[1:], f32),
            in_specs=[vm] * len(other) + [anywhere] * len(after),
            out_specs=vm,
            compiler_params=params,
            name="regroup",
        )(*other, *after)
        return moved + [flip(grouped, 1)]

    there, home = pairing(half, THERE), pairing(half, HOME)
    pieces = pl.pallas_call(
        functools.partial(pack_kernel, nb, tc, tpc, there),
        out_shape=outgoing(there, tpc + EXTRA),
        in_specs=[hbm] * 6,
        out_specs=(hbm,) * len(sends(half, there)),
        scratch_shapes=[
            pltpu.VMEM((ntr, ny, nx), f32),
            pltpu.VMEM((4, ny, nx), f32),
            pltpu.VMEM((ny, nx), jnp.int32),
            pltpu.VMEM((half, EXTRA) + tile, f32),
            pltpu.SemaphoreType.DMA((5 + tc,)),
            pltpu.SemaphoreType.DMA((2, half)),
        ],
        compiler_params=pltpu.CompilerParams(vmem_limit_bytes=PACK_LIMIT),
        name="pack",
    )(tracer, east_flow, north_flow, up_flow, diffusivity, kmt)
    wet, depth, decay = pl.pallas_call(
        functools.partial(prep_kernel, nb, tc, tpc),
        out_shape=(
            struct(half + 1),
            struct(half + 1),
            jax.ShapeDtypeStruct((half, tpc, LANES), f32),
        ),
        in_specs=[sm, sm, sm, vm],
        out_specs=(vm,) * 3,
        compiler_params=params,
        name="prep",
    )(thickness, group, group_rate, kmt)
    kept = pl.pallas_call(
        keep_kernel,
        out_shape=struct(tpc + EXTRA),
        in_specs=[anywhere] * 2,
        out_specs=vm,
        scratch_shapes=[pltpu.SemaphoreType.DMA((1,))],
        compiler_params=params,
        name="keep",
    )(wet, pieces[-1])
    arrived = exchange(pieces[:-1] + (kept,), there)
    evens = half // 2 - 1
    relayed = pl.pallas_call(
        functools.partial(relay_kernel, nb, tc, tpc),
        out_shape=struct(2),
        in_specs=[vm] * (2 + evens),
        out_specs=vm,
        compiler_params=params,
        name="relay",
    )(up_flow, diffusivity, *arrived[:evens])
    own = pl.pallas_call(
        functools.partial(pick_kernel, nb, tc),
        out_shape=struct(2),
        in_specs=[vm, vm],
        out_specs=vm,
        compiler_params=params,
        name="pick",
    )(relayed, flip(relayed, 1))
    other = flip(own, half)
    f, cells, cin, base = pl.pallas_call(
        functools.partial(solve_kernel, nb, tc, tpc, there),
        out_shape=(struct(half, tpc), struct(tpc), struct(half - 1), struct(5)),
        in_specs=[vm] * (3 + len(arrived)),
        out_specs=(vm,) * 4,
        scratch_shapes=[pltpu.VMEM((half, tpc + EXTRA) + tile, f32)],
        compiler_params=params,
        name="solve",
    )(wet, depth, decay, *arrived)
    f_last, coef, message = pl.pallas_call(
        functools.partial(seam_kernel, half, tpc),
        out_shape=(struct(tpc), struct(3), struct(tpc + 1)),
        in_specs=[vm] * 5,
        out_specs=(vm,) * 3,
        compiler_params=params,
        name="seam",
    )(f, cells, base, own, other)
    solved = pl.pallas_call(
        functools.partial(back_kernel, nb, tc, tpc, home),
        out_shape=outgoing(home, tpc),
        in_specs=[vm] * 6,
        out_specs=(vm,) * len(sends(half, home)),
        scratch_shapes=[pltpu.VMEM((half, tpc) + tile, f32)],
        compiler_params=params,
        name="back",
    )(f, cin, f_last, coef, message, flip(message, half))
    back = exchange(solved, home)
    return pl.pallas_call(
        functools.partial(join_kernel, nb, tc, tpc, home),
        out_shape=jax.ShapeDtypeStruct(tracer.shape, f32),
        in_specs=[anywhere] * len(back),
        out_specs=hbm,
        scratch_shapes=[pltpu.SemaphoreType.DMA((half,))],
        compiler_params=params,
        name="join",
    )(*back)


def solution(mesh):
    placed = (
        P(None, "lev", "band", None),
        P("lev", "band", None),
        P("lev", "band", None),
        P("lev", "band", None),
        P("lev", "band", None),
        P(),
        P("band", None),
        P(),
        P(),
    )
    return jax.shard_map(
        shards, mesh=mesh, in_specs=placed, out_specs=P(None, "lev", "band", None), check_vma=False
    )
```

```python
import functools

import jax
import jax.numpy as jnp
from jax import lax
from jax.experimental import pallas as pl
from jax.experimental.pallas import tpu as pltpu
from jax.sharding import PartitionSpec as P

LANES = 128
ROWS = 8
THERE, HOME = "none", "none"
WAIT = 1
EDGE, EAST, NORTH, UP, DIFF, EXTRA = 0, 1, 2, 3, 4, 5
f32 = jnp.float32
VMEM_LIMIT = 16 * 1024 * 1024
PACK_LIMIT = 60 * 1024 * 1024


def lanes_iota():
    return lax.broadcasted_iota(jnp.int32, (ROWS, LANES), 1)


def rows_iota():
    return lax.broadcasted_iota(jnp.int32, (ROWS, LANES), 0)


def devices(half):
    far, near = half // 2, half // 4
    crossed = lambda d: ((d & far) > 0) + ((d & near) > 0)
    return sorted(range(1, half), key=lambda d: (d < 2, d & 1, -crossed(d), -d)) + [0]


def n_extra(d):
    return 1 if d % 2 else EXTRA


def pairing(half, which):
    if which == "none":
        return ()
    far = half // 2 | half // 4
    return tuple(d for d in range(2, half, 2) if which == "all" or d & far == far)


def sends(half, paired):
    order = [(d, d in paired) for d in devices(half) if d > 1 and (d % 2 == 0 or d - 1 not in paired)]
    return order + [(0, True)] if paired else order + [(1, False), (0, False)]


def by_level(half, paired, refs, rank):
    order = sends(half, paired)
    direct = [(rank ^ d, refs[j].at[0] if both else refs[j]) for j, (d, both) in enumerate(order)]
    swapped = [d ^ 1 for d, both in order if both]
    return direct + [(rank ^ d, refs[len(order)].at[j]) for j, d in enumerate(swapped)]


def n_arrived(half, paired):
    return len(sends(half, paired)) + (1 if paired else 0)


def place(nb, tc):
    half = nb * tc
    index = lax.axis_index("lev")
    rank = lax.rem(index, half)
    return lax.div(index, half), rank, lax.div(rank, tc), lax.rem(rank, tc)


def pack_kernel(nb, tc, tpc, odd, tracer, east, north, up, diff, kmt, *refs):
    half = nb * tc
    _, rank, _, chunk = place(nb, tc)
    distances = [d for d in devices(half) if d % 2 == odd]
    turns = range(odd, tc, 2)
    out = dict(zip(distances, refs))
    cells, fields, depth, extra, sem, store_sem = refs[len(distances) :]
    loads = [pltpu.make_async_copy(kmt, depth, sem.at[0])]
    for i, field in enumerate((east,) if odd else (east, north, up, diff)):
        loads.append(pltpu.make_async_copy(field, fields.at[pl.ds(i, 1)], sem.at[1 + i]))
    chunks = [
        pltpu.make_async_copy(
            tracer.at[pl.ds((chunk ^ e) * tpc, tpc), 0], cells.at[pl.ds(e // 2 * tpc, tpc)], sem.at[5 + e // 2]
        )
        for e in turns
    ]
    for copy in chunks + loads:
        copy.start()
    for copy in chunks:
        copy.wait()
    stores = []
    for d in distances:
        cut = pl.ds(pl.multiple_of(lax.div(rank ^ d, tc) * LANES, LANES), LANES)
        copy = pltpu.make_async_copy(
            cells.at[pl.ds(d % tc // 2 * tpc, tpc), :, cut], out[d].at[pl.ds(0, tpc)], store_sem.at[0, d // 2]
        )
        copy.start()
        stores.append(copy)
    for copy in loads:
        copy.wait()
    lane = lanes_iota()
    cols = [slice(b * LANES, (b + 1) * LANES) for b in range(nb)]
    wet = [(lax.axis_index("lev") < depth[:, cols[b]]).astype(f32) for b in range(nb)]
    flow = [None]
    for b in range(1, nb):
        ends = fields[0, :, cols[b - 1]][:, LANES - 1 :]
        ends = ends * wet[b - 1][:, LANES - 1 :] * wet[b][:, :1]
        flow.append(jnp.broadcast_to(ends, (ROWS, LANES)))
    for e in turns:
        faces = [jnp.zeros((ROWS, LANES), f32) for _ in range(nb)]
        for t in range(tpc):
            at = e // 2 * tpc + t
            for b in range(1, nb):
                west = pltpu.roll(cells[at, :, cols[b - 1]], (2 * t + 1) % LANES, 1)
                here = cells[at, :, cols[b]]
                here = pltpu.roll(here, 2 * t, 1) if t else here
                face = jnp.maximum(flow[b], 0.0) * west + jnp.minimum(flow[b], 0.0) * here
                faces[b] = jnp.where(lane == 2 * t, face, faces[b])
        for b in range(nb):
            edge = faces[b]
            if b + 1 < nb:
                edge = edge - pltpu.roll(faces[b + 1], LANES - 1, 1)
            extra[e // 2, b, EDGE] = edge
            if not odd:
                for i in range(4):
                    extra[e // 2, b, EAST + i] = fields[i, :, cols[b]]
    for d in distances:
        copy = pltpu.make_async_copy(
            extra.at[d % tc // 2, lax.div(rank ^ d, tc), pl.ds(0, n_extra(d))],
            out[d].at[pl.ds(tpc, n_extra(d))],
            store_sem.at[1, d // 2],
        )
        copy.start()
        stores.append(copy)
    for copy in stores:
        copy.wait()


def keep_kernel(prepared, piece, own, sem):
    del prepared
    copy = pltpu.make_async_copy(piece, own, sem.at[0])
    copy.start()
    copy.wait()


def relay_kernel(nb, tc, tpc, east, north, up, diff, *refs):
    half = nb * tc
    arrived, (out, seam) = refs[:-2], refs[-2:]
    _, rank, block, _ = place(nb, tc)
    cols = pl.ds(pl.multiple_of(block * LANES, LANES), LANES)
    for j, even in enumerate(arrived):
        for i in range(4):
            out[4 * j + i] = even[tpc + EAST + i]
    own = [level[0, :, cols] for level in (east, north, up, diff)]
    for i in range(4):
        out[4 * len(arrived) + i] = own[i]
    for i in range(2):
        field = own[UP - EAST + i]
        for d, even in zip(devices(half), arrived):
            field = jnp.where(rank == d, even[tpc + UP + i], field)
        out[4 * len(arrived) + 4 + i] = field
        seam[i] = field


def pick_kernel(nb, tc, seam, swapped, own):
    _, rank, _, _ = place(nb, tc)
    for i in range(2):
        own[i] = jnp.where(lax.rem(rank, 2) == 1, swapped[swapped.shape[0] - 2 + i], seam[i])


def prep_kernel(nb, tc, tpc, thickness, group, rates, kmt_all, wet, depth, decay, table):
    half = nb * tc
    upper, _, block, chunk = place(nb, tc)
    kmt = kmt_all[:, pl.ds(pl.multiple_of(block * LANES, LANES), LANES)]
    levels = [jnp.where(upper == 1, 2 * half - 1 - o, o) for o in range(half + 1)]
    for o, k in enumerate(levels):
        wet[o] = (k < kmt).astype(f32)
        depth[o] = jnp.full((ROWS, LANES), thickness[k], f32)
    row = rows_iota()
    for g in range(rates.shape[0]):
        for at in range(0, half, ROWS):
            tile = jnp.zeros((ROWS, LANES), f32)
            for i in range(min(ROWS, half - at)):
                tile = jnp.where(row == i, rates[g, levels[at + i]], tile)
            table[g, at : at + ROWS] = tile[: min(ROWS, half - at)]
    for t in range(tpc):
        decay[t] = table[group[chunk * tpc + t]]


def solve_kernel(nb, tc, tpc, paired, wets, depths, decay, swapped, *refs):
    half = nb * tc
    arrived = refs[: n_arrived(half, paired)]
    f_out, cells_out, cin_out, base_out, got = refs[-5:]
    upper, rank, _, _ = place(nb, tc)
    evens = [d for d in devices(half) if d % 2 == 0]
    for d, piece in zip(devices(half), arrived):
        for t in range(tpc):
            got[rank ^ d, t] = piece[t]
        got[rank ^ d, tpc + EDGE] = piece[tpc + EDGE]
        for i in range(EAST, EXTRA):
            if d % 2:
                got[rank ^ d, tpc + i] = swapped[4 * evens.index(d ^ 1) + i - EAST]
            else:
                got[rank ^ d, tpc + i] = piece[tpc + i]
    sign = 1.0 - 2.0 * upper.astype(f32)
    lane, row = lanes_iota(), rows_iota()
    ends = jnp.logical_or(lane == 0, lane == LANES - 1)

    def slot_of(o):
        return jnp.where(upper == 1, half - 1 - o, o)

    zero = jnp.zeros((ROWS, LANES), f32)
    cin = tout = outer = add_mid = zero
    for o in range(half):
        slot = slot_of(o)
        dz, dz_next = depths[o], depths[o + 1]
        wet, wet_next = wets[o], wets[o + 1]
        last = o + 1 == half
        mid = wet + add_mid
        denom = 1.0 - outer - outer * cin
        if not last:
            face = jnp.where(upper == 1, slot, slot_of(o + 1))
            pos, neg, g = interface(
                got[face, tpc + UP], got[face, tpc + DIFF], sign, wet * wet_next, dz, dz_next
            )
            mid = mid + neg / dz
            tin = pos / dz
            inner = -g / dz
            alpha = 1.0 / (denom - inner)
        east = got[slot, tpc + EAST] * wet * pltpu.roll(wet, LANES - 1, 1)
        east = jnp.where(lane == LANES - 1, 0.0, east)
        north = got[slot, tpc + NORTH] * wet * pltpu.roll(wet, ROWS - 1, 0)
        north = jnp.where(row == ROWS - 1, 0.0, north)
        e_pos, e_neg = jnp.maximum(east, 0.0), jnp.minimum(east, 0.0)
        n_pos, n_neg = jnp.maximum(north, 0.0), jnp.minimum(north, 0.0)
        mid = mid - e_pos - n_pos + pltpu.roll(e_neg, 1, 1) + pltpu.roll(n_neg, 1, 0)
        e_pos, n_pos = pltpu.roll(e_pos, 1, 1), pltpu.roll(n_pos, 1, 0)
        edges = got[slot, tpc + EDGE]
        prev_slot = slot_of(o - 1) if o else None
        next_slot = None if last else slot_of(o + 1)
        for t in range(tpc):
            c = got[slot, t]
            star = c * (mid - decay[t, pl.ds(o, 1)] * wet)
            if o:
                star += tout * got[prev_slot, t]
            if not last:
                star += tin * got[next_slot, t]
            star += e_pos * pltpu.roll(c, 1, 1) - e_neg * pltpu.roll(c, LANES - 1, 1)
            star += n_pos * pltpu.roll(c, 1, 0) - n_neg * pltpu.roll(c, ROWS - 1, 0)
            edge = pltpu.roll(edges, LANES - 2 * t, 1) if t else edges
            star += jnp.where(ends, edge, 0.0)
            if o:
                star -= outer * f_out[o - 1, t]
            f_out[o, t] = star if last else alpha * star
            if last:
                cells_out[t] = c
        if last:
            base_out[0] = denom
            base_out[1] = wet * wet_next
            base_out[2] = jnp.full((ROWS, LANES), sign, f32)
            base_out[3] = dz
            base_out[4] = dz_next
        else:
            cin = inner * alpha
            cin_out[o] = cin
            tout, outer, add_mid = -neg / dz_next, -g / dz_next, -pos / dz_next


def interface(w, g, sign, open_face, dz, dz_next):
    w = sign * w * open_face
    dz_min = jnp.minimum(dz, dz_next)
    g = g * open_face / (0.5 * (dz + dz_next))
    return dz_min * jnp.maximum(w, 0.0), dz_min * jnp.minimum(w, 0.0), g


def seam_kernel(half, count, star, cells, base, own, other, f_out, coef_out, message):
    sign, dz, dz_next = base[2], base[3], base[4]
    w = jnp.where(sign < 0.0, own[0], other[0])
    g = jnp.where(sign < 0.0, own[1], other[1])
    pos, neg, g = interface(w, g, sign, base[1], dz, dz_next)
    inner, outer_next = -g / dz, -g / dz_next
    mid, tout_next = neg / dz, -neg / dz_next
    alpha = 1.0 / (base[0] - inner)
    for t in range(count):
        c = cells[t]
        f = alpha * (star[half - 1, t] + mid * c)
        f_out[t] = f
        message[t] = tout_next * c - outer_next * f
    coef_out[0] = inner * alpha
    coef_out[1] = alpha
    coef_out[2] = outer_next
    message[count] = alpha


def back_kernel(nb, tc, tpc, paired, f_in, cin, f_last, coef, sent, got, *refs):
    half = nb * tc
    out, solved = refs[:-1], refs[-1]
    upper, rank, _, _ = place(nb, tc)
    slots = [jnp.where(upper == 1, half - 1 - o, o) for o in range(half)]
    other = coef[0] * got[tpc]
    scale = 1.0 / (1.0 - other * coef[2])
    mine, theirs = scale * coef[1], scale * other
    for t in range(tpc):
        x = f_last[t] + (mine * got[t] - theirs * sent[t])
        solved[slots[half - 1], t] = x
        for o in range(half - 2, -1, -1):
            x = f_in[o, t] - cin[o] * x
            solved[slots[o], t] = x
    for (d, both), piece in zip(sends(half, paired), out):
        for t in range(tpc):
            if both:
                piece[0, t] = solved[rank ^ d, t]
                piece[1, t] = solved[rank ^ d ^ 1, t]
            else:
                piece[t] = solved[rank ^ d, t]


def join_kernel(nb, tc, tpc, paired, *refs):
    half = nb * tc
    arrived, out, sem = refs[:-2], refs[-2], refs[-1]
    copies = []
    _, rank, _, _ = place(nb, tc)
    for i, (r, piece) in enumerate(by_level(half, paired, arrived, rank)):
        cols = pl.ds(pl.multiple_of(lax.div(r, tc) * LANES, LANES), LANES)
        copies.append(
            pltpu.make_async_copy(
                piece, out.at[pl.ds(lax.rem(r, tc) * tpc, tpc), 0, :, cols], sem.at[i]
            )
        )
    for copy in copies:
        copy.start()
    for copy in copies:
        copy.wait()


def shards(tracer, east_flow, north_flow, up_flow, diffusivity, thickness, kmt, group, group_rate):
    ntr, ldev, ny, nx = tracer.shape
    count = lax.axis_size("lev")
    half = count // 2
    nb = nx // LANES
    tc = half // nb
    tpc = ntr // tc
    assert tc % 2 == 0 and 2 * tpc <= LANES
    assert ldev == 1 and ny == ROWS and nb * LANES == nx and tc * nb == half and tpc * tc == ntr
    tile = (ROWS, LANES)
    vm = pl.BlockSpec(memory_space=pltpu.VMEM)
    sm = pl.BlockSpec(memory_space=pltpu.SMEM)
    hbm = pl.BlockSpec(memory_space=pltpu.HBM)
    anywhere = pl.BlockSpec(memory_space=pl.ANY)
    params = pltpu.CompilerParams(vmem_limit_bytes=VMEM_LIMIT)

    def flip(value, bits):
        return lax.ppermute(value, "lev", [(i, i ^ bits) for i in range(count)])

    def struct(*shape):
        return jax.ShapeDtypeStruct(shape + tile, f32)

    def outgoing(paired, n):
        return tuple(struct(2, n) if both else struct(n) for _, both in sends(half, paired))

    def exchange(values, paired):
        order = sends(half, paired)
        moved = [flip(piece, d) if d else piece for (d, _), piece in zip(order, values)]
        if not paired:
            return moved
        other = [piece for (_, both), piece in zip(order, moved) if both]
        after = [piece for (_, both), piece in zip(order, moved) if not both][:WAIT]
        grouped = pl.pallas_call(
            regroup_kernel,
            out_shape=jax.ShapeDtypeStruct((len(other),) + other[0].shape[1:], f32),
            in_specs=[vm] * len(other) + [anywhere] * len(after),
            out_specs=vm,
            compiler_params=params,
            name="regroup",
        )(*other, *after)
        return moved + [flip(grouped, 1)]

    there, home = pairing(half, THERE), pairing(half, HOME)
    packed = {}
    for odd in range(2):
        distances = [d for d in devices(half) if d % 2 == odd]
        pieces = pl.pallas_call(
            functools.partial(pack_kernel, nb, tc, tpc, odd),
            out_shape=tuple(struct(tpc + n_extra(d)) for d in distances),
            in_specs=[hbm] * 6,
            out_specs=(hbm,) * len(distances),
            scratch_shapes=[
                pltpu.VMEM((ntr // 2, ny, nx), f32),
                pltpu.VMEM((4, ny, nx), f32),
                pltpu.VMEM((ny, nx), jnp.int32),
                pltpu.VMEM((tc // 2, nb, EXTRA) + tile, f32),
                pltpu.SemaphoreType.DMA((5 + tc // 2,)),
                pltpu.SemaphoreType.DMA((2, half // 2)),
            ],
            compiler_params=pltpu.CompilerParams(vmem_limit_bytes=PACK_LIMIT),
            name="pack",
        )(tracer, east_flow, north_flow, up_flow, diffusivity, kmt)
        packed.update(zip(distances, pieces))
    pieces = tuple(packed[d] for d in devices(half))
    wet, depth, decay = pl.pallas_call(
        functools.partial(prep_kernel, nb, tc, tpc),
        out_shape=(
            struct(half + 1),
            struct(half + 1),
            jax.ShapeDtypeStruct((tpc, half, LANES), f32),
        ),
        in_specs=[sm, sm, sm, vm],
        out_specs=(vm,) * 3,
        scratch_shapes=[pltpu.VMEM((group_rate.shape[0], half, LANES), f32)],
        compiler_params=params,
        name="prep",
    )(thickness, group, group_rate, kmt)
    kept = pl.pallas_call(
        keep_kernel,
        out_shape=struct(tpc + EXTRA),
        in_specs=[anywhere] * 2,
        out_specs=vm,
        scratch_shapes=[pltpu.SemaphoreType.DMA((1,))],
        compiler_params=params,
        name="keep",
    )(wet, pieces[-1])
    arrived = exchange(pieces[:-1] + (kept,), there)
    evens = half // 2 - 1
    relayed, seam = pl.pallas_call(
        functools.partial(relay_kernel, nb, tc, tpc),
        out_shape=(struct(4 * (evens + 1) + 2), struct(2)),
        in_specs=[vm] * (4 + evens),
        out_specs=(vm, vm),
        compiler_params=params,
        name="relay",
    )(east_flow, north_flow, up_flow, diffusivity, *arrived[:evens])
    swapped = flip(relayed, 1)
    own = pl.pallas_call(
        functools.partial(pick_kernel, nb, tc),
        out_shape=struct(2),
        in_specs=[vm, vm],
        out_specs=vm,
        compiler_params=params,
        name="pick",
    )(seam, swapped)
    other = flip(own, half)
    f, cells, cin, base = pl.pallas_call(
        functools.partial(solve_kernel, nb, tc, tpc, there),
        out_shape=(struct(half, tpc), struct(tpc), struct(half - 1), struct(5)),
        in_specs=[vm] * (4 + len(arrived)),
        out_specs=(vm,) * 4,
        scratch_shapes=[pltpu.VMEM((half, tpc + EXTRA) + tile, f32)],
        compiler_params=params,
        name="solve",
    )(wet, depth, decay, swapped, *arrived)
    f_last, coef, message = pl.pallas_call(
        functools.partial(seam_kernel, half, tpc),
        out_shape=(struct(tpc), struct(3), struct(tpc + 1)),
        in_specs=[vm] * 5,
        out_specs=(vm,) * 3,
        compiler_params=params,
        name="seam",
    )(f, cells, base, own, other)
    solved = pl.pallas_call(
        functools.partial(back_kernel, nb, tc, tpc, home),
        out_shape=outgoing(home, tpc),
        in_specs=[vm] * 6,
        out_specs=(vm,) * len(sends(half, home)),
        scratch_shapes=[pltpu.VMEM((half, tpc) + tile, f32)],
        compiler_params=params,
        name="back",
    )(f, cin, f_last, coef, message, flip(message, half))
    back = exchange(solved, home)
    return pl.pallas_call(
        functools.partial(join_kernel, nb, tc, tpc, home),
        out_shape=jax.ShapeDtypeStruct(tracer.shape, f32),
        in_specs=[anywhere] * len(back),
        out_specs=hbm,
        scratch_shapes=[pltpu.SemaphoreType.DMA((half,))],
        compiler_params=params,
        name="join",
    )(*back)


def solution(mesh):
    placed = (
        P(None, "lev", "band", None),
        P("lev", "band", None),
        P("lev", "band", None),
        P("lev", "band", None),
        P("lev", "band", None),
        P(),
        P("band", None),
        P(),
        P(),
    )
    return jax.shard_map(
        shards, mesh=mesh, in_specs=placed, out_specs=P(None, "lev", "band", None), check_vma=False
    )
```

```python
import functools

import jax
import jax.numpy as jnp
from jax import lax
from jax.experimental import pallas as pl
from jax.experimental.pallas import tpu as pltpu
from jax.sharding import PartitionSpec as P

LANES = 128
ROWS = 8
THERE, HOME = "none", "none"
WAIT = 1
EDGE, EAST, NORTH, UP, DIFF, EXTRA = 0, 1, 2, 3, 4, 5
f32 = jnp.float32
VMEM_LIMIT = 16 * 1024 * 1024
PACK_LIMIT = 60 * 1024 * 1024


def lanes_iota():
    return lax.broadcasted_iota(jnp.int32, (ROWS, LANES), 1)


def rows_iota():
    return lax.broadcasted_iota(jnp.int32, (ROWS, LANES), 0)


def devices(half):
    far, near = half // 2, half // 4
    crossed = lambda d: ((d & far) > 0) + ((d & near) > 0)
    return sorted(range(1, half), key=lambda d: (d < 2, d & 1, -crossed(d), -d)) + [0]


def n_extra(d):
    return 1 if d % 2 else EXTRA


def pairing(half, which):
    if which == "none":
        return ()
    far = half // 2 | half // 4
    return tuple(d for d in range(2, half, 2) if which == "all" or d & far == far)


def sends(half, paired):
    order = [(d, d in paired) for d in devices(half) if d > 1 and (d % 2 == 0 or d - 1 not in paired)]
    return order + [(0, True)] if paired else order + [(1, False), (0, False)]


def by_level(half, paired, refs, rank):
    order = sends(half, paired)
    direct = [(rank ^ d, refs[j].at[0] if both else refs[j]) for j, (d, both) in enumerate(order)]
    swapped = [d ^ 1 for d, both in order if both]
    return direct + [(rank ^ d, refs[len(order)].at[j]) for j, d in enumerate(swapped)]


def n_arrived(half, paired):
    return len(sends(half, paired)) + (1 if paired else 0)


def place(nb, tc):
    half = nb * tc
    index = lax.axis_index("lev")
    rank = lax.rem(index, half)
    return lax.div(index, half), rank, lax.div(rank, tc), lax.rem(rank, tc)


def pack_kernel(nb, tc, tpc, odd, tracer, east, north, up, diff, kmt, *refs):
    half = nb * tc
    _, rank, _, chunk = place(nb, tc)
    distances = [d for d in devices(half) if d % 2 == odd]
    turns = range(odd, tc, 2)
    out = dict(zip(distances, refs))
    cells, fields, depth, extra, sem, store_sem = refs[len(distances) :]
    loads = [pltpu.make_async_copy(kmt, depth, sem.at[0])]
    for i, field in enumerate((east,) if odd else (east, north, up, diff)):
        loads.append(pltpu.make_async_copy(field, fields.at[pl.ds(i, 1)], sem.at[1 + i]))
    chunks = [
        pltpu.make_async_copy(
            tracer.at[pl.ds((chunk ^ e) * tpc, tpc), 0], cells.at[pl.ds(e // 2 * tpc, tpc)], sem.at[5 + e // 2]
        )
        for e in turns
    ]
    for copy in chunks + loads:
        copy.start()
    stores = []
    for d in distances:
        cut = pl.ds(pl.multiple_of(lax.div(rank ^ d, tc) * LANES, LANES), LANES)
        copy = pltpu.make_async_copy(
            tracer.at[pl.ds((chunk ^ d % tc) * tpc, tpc), 0, :, cut], out[d].at[pl.ds(0, tpc)], store_sem.at[d // 2]
        )
        copy.start()
        stores.append(copy)
    for copy in chunks + loads:
        copy.wait()
    lane = lanes_iota()
    cols = [slice(b * LANES, (b + 1) * LANES) for b in range(nb)]
    wet = [(lax.axis_index("lev") < depth[:, cols[b]]).astype(f32) for b in range(nb)]
    flow = [None]
    for b in range(1, nb):
        ends = fields[0, :, cols[b - 1]][:, LANES - 1 :]
        ends = ends * wet[b - 1][:, LANES - 1 :] * wet[b][:, :1]
        flow.append(jnp.broadcast_to(ends, (ROWS, LANES)))
    for e in turns:
        faces = [jnp.zeros((ROWS, LANES), f32) for _ in range(nb)]
        for t in range(tpc):
            at = e // 2 * tpc + t
            for b in range(1, nb):
                west = pltpu.roll(cells[at, :, cols[b - 1]], (2 * t + 1) % LANES, 1)
                here = cells[at, :, cols[b]]
                here = pltpu.roll(here, 2 * t, 1) if t else here
                face = jnp.maximum(flow[b], 0.0) * west + jnp.minimum(flow[b], 0.0) * here
                faces[b] = jnp.where(lane == 2 * t, face, faces[b])
        for b in range(nb):
            edge = faces[b]
            if b + 1 < nb:
                edge = edge - pltpu.roll(faces[b + 1], LANES - 1, 1)
            extra[e // 2, b] = edge
    for d in distances:
        block = lax.div(rank ^ d, tc)
        cut = pl.ds(pl.multiple_of(block * LANES, LANES), LANES)
        out[d][tpc + EDGE] = extra[d % tc // 2, block]
        if not odd:
            for i in range(4):
                out[d][tpc + EAST + i] = fields[i, :, cut]
    for copy in stores:
        copy.wait()


def relay_kernel(nb, tc, tpc, east, north, up, diff, *refs):
    half = nb * tc
    arrived, (out, seam) = refs[:-2], refs[-2:]
    _, rank, block, _ = place(nb, tc)
    cols = pl.ds(pl.multiple_of(block * LANES, LANES), LANES)
    for j, even in enumerate(arrived):
        for i in range(4):
            out[4 * j + i] = even[tpc + EAST + i]
    own = [level[0, :, cols] for level in (east, north, up, diff)]
    for i in range(4):
        out[4 * len(arrived) + i] = own[i]
    for i in range(2):
        field = own[UP - EAST + i]
        for d, even in zip(devices(half), arrived):
            field = jnp.where(rank == d, even[tpc + UP + i], field)
        out[4 * len(arrived) + 4 + i] = field
        seam[i] = field


def pick_kernel(nb, tc, seam, swapped, own):
    _, rank, _, _ = place(nb, tc)
    for i in range(2):
        own[i] = jnp.where(lax.rem(rank, 2) == 1, swapped[swapped.shape[0] - 2 + i], seam[i])


def prep_kernel(nb, tc, tpc, thickness, group, rates, kmt_all, wet, depth, decay, table):
    half = nb * tc
    upper, _, block, chunk = place(nb, tc)
    kmt = kmt_all[:, pl.ds(pl.multiple_of(block * LANES, LANES), LANES)]
    levels = [jnp.where(upper == 1, 2 * half - 1 - o, o) for o in range(half + 1)]
    for o, k in enumerate(levels):
        wet[o] = (k < kmt).astype(f32)
        depth[o] = jnp.full((ROWS, LANES), thickness[k], f32)
    row = rows_iota()
    for g in range(rates.shape[0]):
        for at in range(0, half, ROWS):
            tile = jnp.zeros((ROWS, LANES), f32)
            for i in range(min(ROWS, half - at)):
                tile = jnp.where(row == i, rates[g, levels[at + i]], tile)
            table[g, at : at + ROWS] = tile[: min(ROWS, half - at)]
    for t in range(tpc):
        decay[t] = table[group[chunk * tpc + t]]


def solve_kernel(nb, tc, tpc, paired, wets, depths, decay, swapped, *refs):
    half = nb * tc
    arrived = refs[: n_arrived(half, paired)]
    f_out, cells_out, cin_out, base_out, got = refs[-5:]
    upper, rank, _, _ = place(nb, tc)
    evens = [d for d in devices(half) if d % 2 == 0]
    for d, piece in zip(devices(half), arrived):
        for t in range(tpc):
            got[rank ^ d, t] = piece[t]
        got[rank ^ d, tpc + EDGE] = piece[tpc + EDGE]
        for i in range(EAST, EXTRA):
            if d % 2:
                got[rank ^ d, tpc + i] = swapped[4 * evens.index(d ^ 1) + i - EAST]
            else:
                got[rank ^ d, tpc + i] = piece[tpc + i]
    sign = 1.0 - 2.0 * upper.astype(f32)
    lane, row = lanes_iota(), rows_iota()
    ends = jnp.logical_or(lane == 0, lane == LANES - 1)

    def slot_of(o):
        return jnp.where(upper == 1, half - 1 - o, o)

    zero = jnp.zeros((ROWS, LANES), f32)
    cin = tout = outer = add_mid = zero
    for o in range(half):
        slot = slot_of(o)
        dz, dz_next = depths[o], depths[o + 1]
        wet, wet_next = wets[o], wets[o + 1]
        last = o + 1 == half
        mid = wet + add_mid
        denom = 1.0 - outer - outer * cin
        if not last:
            face = jnp.where(upper == 1, slot, slot_of(o + 1))
            pos, neg, g = interface(
                got[face, tpc + UP], got[face, tpc + DIFF], sign, wet * wet_next, dz, dz_next
            )
            mid = mid + neg / dz
            tin = pos / dz
            inner = -g / dz
            alpha = 1.0 / (denom - inner)
        east = got[slot, tpc + EAST] * wet * pltpu.roll(wet, LANES - 1, 1)
        east = jnp.where(lane == LANES - 1, 0.0, east)
        north = got[slot, tpc + NORTH] * wet * pltpu.roll(wet, ROWS - 1, 0)
        north = jnp.where(row == ROWS - 1, 0.0, north)
        e_pos, e_neg = jnp.maximum(east, 0.0), jnp.minimum(east, 0.0)
        n_pos, n_neg = jnp.maximum(north, 0.0), jnp.minimum(north, 0.0)
        mid = mid - e_pos - n_pos + pltpu.roll(e_neg, 1, 1) + pltpu.roll(n_neg, 1, 0)
        e_pos, n_pos = pltpu.roll(e_pos, 1, 1), pltpu.roll(n_pos, 1, 0)
        edges = got[slot, tpc + EDGE]
        prev_slot = slot_of(o - 1) if o else None
        next_slot = None if last else slot_of(o + 1)
        for t in range(tpc):
            c = got[slot, t]
            star = c * (mid - decay[t, pl.ds(o, 1)] * wet)
            if o:
                star += tout * got[prev_slot, t]
            if not last:
                star += tin * got[next_slot, t]
            star += e_pos * pltpu.roll(c, 1, 1) - e_neg * pltpu.roll(c, LANES - 1, 1)
            star += n_pos * pltpu.roll(c, 1, 0) - n_neg * pltpu.roll(c, ROWS - 1, 0)
            edge = pltpu.roll(edges, LANES - 2 * t, 1) if t else edges
            star += jnp.where(ends, edge, 0.0)
            if o:
                star -= outer * f_out[o - 1, t]
            f_out[o, t] = star if last else alpha * star
            if last:
                cells_out[t] = c
        if last:
            base_out[0] = denom
            base_out[1] = wet * wet_next
            base_out[2] = jnp.full((ROWS, LANES), sign, f32)
            base_out[3] = dz
            base_out[4] = dz_next
        else:
            cin = inner * alpha
            cin_out[o] = cin
            tout, outer, add_mid = -neg / dz_next, -g / dz_next, -pos / dz_next


def interface(w, g, sign, open_face, dz, dz_next):
    w = sign * w * open_face
    dz_min = jnp.minimum(dz, dz_next)
    g = g * open_face / (0.5 * (dz + dz_next))
    return dz_min * jnp.maximum(w, 0.0), dz_min * jnp.minimum(w, 0.0), g


def seam_kernel(half, count, star, cells, base, own, other, f_out, coef_out, message):
    sign, dz, dz_next = base[2], base[3], base[4]
    w = jnp.where(sign < 0.0, own[0], other[0])
    g = jnp.where(sign < 0.0, own[1], other[1])
    pos, neg, g = interface(w, g, sign, base[1], dz, dz_next)
    inner, outer_next = -g / dz, -g / dz_next
    mid, tout_next = neg / dz, -neg / dz_next
    alpha = 1.0 / (base[0] - inner)
    for t in range(count):
        c = cells[t]
        f = alpha * (star[half - 1, t] + mid * c)
        f_out[t] = f
        message[t] = tout_next * c - outer_next * f
    coef_out[0] = inner * alpha
    coef_out[1] = alpha
    coef_out[2] = outer_next
    message[count] = alpha


def back_kernel(nb, tc, tpc, paired, f_in, cin, f_last, coef, sent, got, *refs):
    half = nb * tc
    out, solved = refs[:-1], refs[-1]
    upper, rank, _, _ = place(nb, tc)
    slots = [jnp.where(upper == 1, half - 1 - o, o) for o in range(half)]
    other = coef[0] * got[tpc]
    scale = 1.0 / (1.0 - other * coef[2])
    mine, theirs = scale * coef[1], scale * other
    for t in range(tpc):
        x = f_last[t] + (mine * got[t] - theirs * sent[t])
        solved[slots[half - 1], t] = x
        for o in range(half - 2, -1, -1):
            x = f_in[o, t] - cin[o] * x
            solved[slots[o], t] = x
    for (d, both), piece in zip(sends(half, paired), out):
        for t in range(tpc):
            if both:
                piece[0, t] = solved[rank ^ d, t]
                piece[1, t] = solved[rank ^ d ^ 1, t]
            else:
                piece[t] = solved[rank ^ d, t]


def join_kernel(nb, tc, tpc, paired, *refs):
    half = nb * tc
    arrived, out, sem = refs[:-2], refs[-2], refs[-1]
    copies = []
    _, rank, _, _ = place(nb, tc)
    for i, (r, piece) in enumerate(by_level(half, paired, arrived, rank)):
        cols = pl.ds(pl.multiple_of(lax.div(r, tc) * LANES, LANES), LANES)
        copies.append(
            pltpu.make_async_copy(
                piece, out.at[pl.ds(lax.rem(r, tc) * tpc, tpc), 0, :, cols], sem.at[i]
            )
        )
    for copy in copies:
        copy.start()
    for copy in copies:
        copy.wait()


def shards(tracer, east_flow, north_flow, up_flow, diffusivity, thickness, kmt, group, group_rate):
    ntr, ldev, ny, nx = tracer.shape
    count = lax.axis_size("lev")
    half = count // 2
    nb = nx // LANES
    tc = half // nb
    tpc = ntr // tc
    assert tc % 2 == 0 and 2 * tpc <= LANES
    assert ldev == 1 and ny == ROWS and nb * LANES == nx and tc * nb == half and tpc * tc == ntr
    tile = (ROWS, LANES)
    vm = pl.BlockSpec(memory_space=pltpu.VMEM)
    sm = pl.BlockSpec(memory_space=pltpu.SMEM)
    hbm = pl.BlockSpec(memory_space=pltpu.HBM)
    anywhere = pl.BlockSpec(memory_space=pl.ANY)
    params = pltpu.CompilerParams(vmem_limit_bytes=VMEM_LIMIT)

    def flip(value, bits):
        return lax.ppermute(value, "lev", [(i, i ^ bits) for i in range(count)])

    def struct(*shape):
        return jax.ShapeDtypeStruct(shape + tile, f32)

    def outgoing(paired, n):
        return tuple(struct(2, n) if both else struct(n) for _, both in sends(half, paired))

    def exchange(values, paired):
        order = sends(half, paired)
        moved = [flip(piece, d) if d else piece for (d, _), piece in zip(order, values)]
        if not paired:
            return moved
        other = [piece for (_, both), piece in zip(order, moved) if both]
        after = [piece for (_, both), piece in zip(order, moved) if not both][:WAIT]
        grouped = pl.pallas_call(
            regroup_kernel,
            out_shape=jax.ShapeDtypeStruct((len(other),) + other[0].shape[1:], f32),
            in_specs=[vm] * len(other) + [anywhere] * len(after),
            out_specs=vm,
            compiler_params=params,
            name="regroup",
        )(*other, *after)
        return moved + [flip(grouped, 1)]

    there, home = pairing(half, THERE), pairing(half, HOME)
    packed = {}
    held = [
        pltpu.with_memory_space_constraint(value, pltpu.HBM)
        for value in (tracer, east_flow, north_flow, up_flow, diffusivity, kmt)
    ]
    for odd in range(2):
        distances = [d for d in devices(half) if d % 2 == odd]
        pieces = pl.pallas_call(
            functools.partial(pack_kernel, nb, tc, tpc, odd),
            out_shape=tuple(pltpu.VMEM((tpc + n_extra(d),) + tile, f32) for d in distances),
            in_specs=[hbm] * 6,
            out_specs=(vm,) * len(distances),
            scratch_shapes=[
                pltpu.VMEM((ntr // 2, ny, nx), f32),
                pltpu.VMEM((4, ny, nx), f32),
                pltpu.VMEM((ny, nx), jnp.int32),
                pltpu.VMEM((tc // 2, nb) + tile, f32),
                pltpu.SemaphoreType.DMA((5 + tc // 2,)),
                pltpu.SemaphoreType.DMA((half // 2,)),
            ],
            compiler_params=params,
            name="pack",
        )(*held)
        packed.update(zip(distances, pieces))
    pieces = tuple(packed[d] for d in devices(half))
    wet, depth, decay = pl.pallas_call(
        functools.partial(prep_kernel, nb, tc, tpc),
        out_shape=(
            struct(half + 1),
            struct(half + 1),
            jax.ShapeDtypeStruct((tpc, half, LANES), f32),
        ),
        in_specs=[sm, sm, sm, vm],
        out_specs=(vm,) * 3,
        scratch_shapes=[pltpu.VMEM((group_rate.shape[0], half, LANES), f32)],
        compiler_params=params,
        name="prep",
    )(thickness, group, group_rate, kmt)
    arrived = exchange(pieces, there)
    evens = half // 2 - 1
    relayed, seam = pl.pallas_call(
        functools.partial(relay_kernel, nb, tc, tpc),
        out_shape=(struct(4 * (evens + 1) + 2), struct(2)),
        in_specs=[vm] * (4 + evens),
        out_specs=(vm, vm),
        compiler_params=params,
        name="relay",
    )(east_flow, north_flow, up_flow, diffusivity, *arrived[:evens])
    swapped = flip(relayed, 1)
    own = pl.pallas_call(
        functools.partial(pick_kernel, nb, tc),
        out_shape=struct(2),
        in_specs=[vm, vm],
        out_specs=vm,
        compiler_params=params,
        name="pick",
    )(seam, swapped)
    other = flip(own, half)
    f, cells, cin, base = pl.pallas_call(
        functools.partial(solve_kernel, nb, tc, tpc, there),
        out_shape=(struct(half, tpc), struct(tpc), struct(half - 1), struct(5)),
        in_specs=[vm] * (4 + len(arrived)),
        out_specs=(vm,) * 4,
        scratch_shapes=[pltpu.VMEM((half, tpc + EXTRA) + tile, f32)],
        compiler_params=params,
        name="solve",
    )(wet, depth, decay, swapped, *arrived)
    f_last, coef, message = pl.pallas_call(
        functools.partial(seam_kernel, half, tpc),
        out_shape=(struct(tpc), struct(3), struct(tpc + 1)),
        in_specs=[vm] * 5,
        out_specs=(vm,) * 3,
        compiler_params=params,
        name="seam",
    )(f, cells, base, own, other)
    solved = pl.pallas_call(
        functools.partial(back_kernel, nb, tc, tpc, home),
        out_shape=outgoing(home, tpc),
        in_specs=[vm] * 6,
        out_specs=(vm,) * len(sends(half, home)),
        scratch_shapes=[pltpu.VMEM((half, tpc) + tile, f32)],
        compiler_params=params,
        name="back",
    )(f, cin, f_last, coef, message, flip(message, half))
    back = exchange(solved, home)
    return pl.pallas_call(
        functools.partial(join_kernel, nb, tc, tpc, home),
        out_shape=jax.ShapeDtypeStruct(tracer.shape, f32),
        in_specs=[anywhere] * len(back),
        out_specs=hbm,
        scratch_shapes=[pltpu.SemaphoreType.DMA((half,))],
        compiler_params=params,
        name="join",
    )(*back)


def solution(mesh):
    placed = (
        P(None, "lev", "band", None),
        P("lev", "band", None),
        P("lev", "band", None),
        P("lev", "band", None),
        P("lev", "band", None),
        P(),
        P("band", None),
        P(),
        P(),
    )
    return jax.shard_map(
        shards, mesh=mesh, in_specs=placed, out_specs=P(None, "lev", "band", None), check_vma=False
    )
```

```python
import functools

import jax
import jax.numpy as jnp
from jax import lax
from jax.experimental import pallas as pl
from jax.experimental.pallas import tpu as pltpu
from jax.sharding import PartitionSpec as P

LANES = 128
ROWS = 8
MID, TOUT, TIN, OUTER, ALPHA = range(5)
EDGE, EAST, NORTH, UP, DIFF, EXTRA = 0, 1, 2, 3, 4, 5
f32 = jnp.float32
VMEM_LIMIT = 16 * 1024 * 1024


def lanes_iota():
    return lax.broadcasted_iota(jnp.int32, (ROWS, LANES), 1)


def rows_iota():
    return lax.broadcasted_iota(jnp.int32, (ROWS, LANES), 0)


def crossed(half, d):
    return (d & half // 2 > 0) + (d & half // 4 > 0)


def devices(half):
    return sorted(range(1, half), key=lambda d: (d < 2, d & 1, -crossed(half, d), -d)) + [0]


def homeward(half):
    return sorted(range(1, half), key=lambda d: (d < 2, d & 1, crossed(half, d) * (2 * (d & 1) - 1), -d)) + [0]


def early(half):
    return [d for d in devices(half) if d < 2 or d % 2 == 0]


def n_extra(d):
    return 1 if d % 2 else EXTRA


def place(nb, tc):
    half = nb * tc
    index = lax.axis_index("lev")
    rank = lax.rem(index, half)
    return lax.div(index, half), rank, lax.div(rank, tc), lax.rem(rank, tc)


def pack_kernel(nb, tc, tpc, odd, tracer, east, north, up, diff, kmt, *refs):
    half = nb * tc
    _, rank, _, chunk = place(nb, tc)
    distances = [d for d in devices(half) if d % 2 == odd]
    turns = range(odd, tc, 2)
    scalars, refs = refs[: 3 * odd], refs[3 * odd :]
    out, ready = dict(zip(distances, refs)), refs[len(distances) : -7]
    cells, fields, depth, extra, table, sem, store_sem = refs[-7:]
    loads = [pltpu.make_async_copy(kmt, depth, sem.at[0])]
    for i, field in enumerate((east,) if odd else (east, north, up, diff)):
        loads.append(pltpu.make_async_copy(field, fields.at[pl.ds(i, 1)], sem.at[1 + i]))
    chunks = [
        pltpu.make_async_copy(
            tracer.at[pl.ds((chunk ^ e) * tpc, tpc), 0], cells.at[pl.ds(e // 2 * tpc, tpc)], sem.at[5 + e // 2]
        )
        for e in turns
    ]
    for copy in chunks + loads:
        copy.start()
    stores = []
    for d in distances:
        cut = pl.ds(pl.multiple_of(lax.div(rank ^ d, tc) * LANES, LANES), LANES)
        copy = pltpu.make_async_copy(
            tracer.at[pl.ds((chunk ^ d % tc) * tpc, tpc), 0, :, cut], out[d].at[pl.ds(0, tpc)], store_sem.at[d // 2]
        )
        copy.start()
        stores.append(copy)
    for copy in loads:
        copy.wait()
    if odd:
        prepare(nb, tc, tpc, *scalars, depth, *ready, table)
    for copy in chunks:
        copy.wait()
    lane = lanes_iota()
    cols = [slice(b * LANES, (b + 1) * LANES) for b in range(nb)]
    wet = [(lax.axis_index("lev") < depth[:, cols[b]]).astype(f32) for b in range(nb)]
    flow = [None]
    for b in range(1, nb):
        ends = fields[0, :, cols[b - 1]][:, LANES - 1 :]
        ends = ends * wet[b - 1][:, LANES - 1 :] * wet[b][:, :1]
        flow.append(jnp.broadcast_to(ends, (ROWS, LANES)))
    for e in turns:
        faces = [jnp.zeros((ROWS, LANES), f32) for _ in range(nb)]
        for t in range(tpc):
            at = e // 2 * tpc + t
            for b in range(1, nb):
                west = pltpu.roll(cells[at, :, cols[b - 1]], (2 * t + 1) % LANES, 1)
                here = cells[at, :, cols[b]]
                here = pltpu.roll(here, 2 * t, 1) if t else here
                face = jnp.maximum(flow[b], 0.0) * west + jnp.minimum(flow[b], 0.0) * here
                faces[b] = jnp.where(lane == 2 * t, face, faces[b])
        for b in range(nb):
            edge = faces[b]
            if b + 1 < nb:
                edge = edge - pltpu.roll(faces[b + 1], LANES - 1, 1)
            extra[e // 2, b] = edge
    for d in distances:
        block = lax.div(rank ^ d, tc)
        cut = pl.ds(pl.multiple_of(block * LANES, LANES), LANES)
        out[d][tpc + EDGE] = extra[d % tc // 2, block]
        if not odd:
            for i in range(4):
                out[d][tpc + EAST + i] = fields[i, :, cut]
    for copy in stores:
        copy.wait()


def relay_kernel(nb, tc, tpc, east, north, up, diff, *refs):
    half = nb * tc
    arrived, (out, seam) = refs[:-2], refs[-2:]
    _, rank, block, _ = place(nb, tc)
    cols = pl.ds(pl.multiple_of(block * LANES, LANES), LANES)
    for j, even in enumerate(arrived):
        for i in range(4):
            out[4 * j + i] = even[tpc + EAST + i]
    own = [level[0, :, cols] for level in (east, north, up, diff)]
    for i in range(4):
        out[4 * len(arrived) + i] = own[i]
    for i in range(2):
        field = own[UP - EAST + i]
        for d, even in zip(devices(half), arrived):
            field = jnp.where(rank == d, even[tpc + UP + i], field)
        out[4 * len(arrived) + 4 + i] = field
        seam[i] = field


def pick_kernel(nb, tc, seam, swapped, own):
    _, rank, _, _ = place(nb, tc)
    for i in range(2):
        own[i] = jnp.where(lax.rem(rank, 2) == 1, swapped[swapped.shape[0] - 2 + i], seam[i])


def prepare(nb, tc, tpc, thickness, group, rates, kmt_all, wet, depth, decay, table):
    half = nb * tc
    upper, _, block, chunk = place(nb, tc)
    kmt = kmt_all[:, pl.ds(pl.multiple_of(block * LANES, LANES), LANES)]
    levels = [jnp.where(upper == 1, 2 * half - 1 - o, o) for o in range(half + 1)]
    for o, k in enumerate(levels):
        wet[o] = (k < kmt).astype(f32)
        depth[o] = jnp.full((ROWS, LANES), thickness[k], f32)
    row = rows_iota()
    for g in range(rates.shape[0]):
        for at in range(0, half, ROWS):
            tile = jnp.zeros((ROWS, LANES), f32)
            for i in range(min(ROWS, half - at)):
                tile = jnp.where(row == i, rates[g, levels[at + i]], tile)
            table[g, at : at + ROWS] = tile[: min(ROWS, half - at)]
    for t in range(tpc):
        decay[t] = table[group[chunk * tpc + t]]


def horizontal(half, tpc, d, piece, fields, rank, upper, wets, decay, cells, sums):
    lane, row = lanes_iota(), rows_iota()
    ends = jnp.logical_or(lane == 0, lane == LANES - 1)
    slot = rank ^ d
    o = jnp.where(upper == 1, half - 1 - slot, slot)
    wet = wets[o]
    east = fields[0] * wet * pltpu.roll(wet, LANES - 1, 1)
    east = jnp.where(lane == LANES - 1, 0.0, east)
    north = fields[1] * wet * pltpu.roll(wet, ROWS - 1, 0)
    north = jnp.where(row == ROWS - 1, 0.0, north)
    e_pos, e_neg = jnp.maximum(east, 0.0), jnp.minimum(east, 0.0)
    n_pos, n_neg = jnp.maximum(north, 0.0), jnp.minimum(north, 0.0)
    mid = wet - e_pos - n_pos + pltpu.roll(e_neg, 1, 1) + pltpu.roll(n_neg, 1, 0)
    e_pos, n_pos = pltpu.roll(e_pos, 1, 1), pltpu.roll(n_pos, 1, 0)
    edges = piece[tpc + EDGE]
    for t in range(tpc):
        c = piece[t]
        star = c * (mid - decay[t, pl.ds(o, 1)] * wet)
        star += e_pos * pltpu.roll(c, 1, 1) - e_neg * pltpu.roll(c, LANES - 1, 1)
        star += n_pos * pltpu.roll(c, 1, 0) - n_neg * pltpu.roll(c, ROWS - 1, 0)
        edge = pltpu.roll(edges, LANES - 2 * t, 1) if t else edges
        cells[slot, t] = c
        sums[slot, t] = star + jnp.where(ends, edge, 0.0)


def field_of(half, tpc, d, pieces, swapped):
    evens = [e for e in devices(half) if e % 2 == 0]
    if d % 2 == 0:
        return [pieces[d][tpc + EAST + i] for i in range(4)]
    return [swapped[4 * evens.index(d ^ 1) + i] for i in range(4)]


def first_kernel(nb, tc, tpc, wets, depths, decay, swapped, *refs):
    half = nb * tc
    pieces = dict(zip(early(half), refs))
    cells, sums, coef, cin_out, base, vertical = refs[len(pieces) :]
    upper, rank, _, _ = place(nb, tc)
    sign = 1.0 - 2.0 * upper.astype(f32)
    for d in range(half):
        fields = field_of(half, tpc, d, pieces, swapped)
        vertical[rank ^ d, 0], vertical[rank ^ d, 1] = fields[2], fields[3]
        if d in pieces:
            horizontal(half, tpc, d, pieces[d], fields, rank, upper, wets, decay, cells, sums)

    def slot_of(o):
        return jnp.where(upper == 1, half - 1 - o, o)

    zero = jnp.zeros((ROWS, LANES), f32)
    cin = tout = outer = mid = zero
    for o in range(half):
        dz, dz_next = depths[o], depths[o + 1]
        open_face = wets[o] * wets[o + 1]
        denom = 1.0 - outer - outer * cin
        coef[o, TOUT], coef[o, OUTER] = tout, outer
        if o + 1 == half:
            coef[o, MID] = mid
            base[0], base[1], base[3], base[4] = denom, open_face, dz, dz_next
            base[2] = jnp.full((ROWS, LANES), sign, f32)
        else:
            face = jnp.where(upper == 1, slot_of(o), slot_of(o + 1))
            pos, neg, g = interface(vertical[face, 0], vertical[face, 1], sign, open_face, dz, dz_next)
            inner = -g / dz
            alpha = 1.0 / (denom - inner)
            cin = inner * alpha
            coef[o, MID], coef[o, TIN], coef[o, ALPHA] = mid + neg / dz, pos / dz, alpha
            cin_out[o] = cin
            tout, outer, mid = -neg / dz_next, -g / dz_next, -pos / dz_next


def solve_kernel(nb, tc, tpc, wets, decay, swapped, coef, *refs):
    half = nb * tc
    late = [d for d in devices(half) if d not in early(half)]
    pieces = dict(zip(late, refs))
    cells, sums, f_out = refs[-3:]
    upper, rank, _, _ = place(nb, tc)
    for d in late:
        fields = field_of(half, tpc, d, pieces, swapped)
        horizontal(half, tpc, d, pieces[d], fields, rank, upper, wets, decay, cells, sums)
    for o in range(half):
        slot, before, after = [jnp.where(upper == 1, half - 1 - k, k) for k in (o, o - 1, o + 1)]
        for t in range(tpc):
            star = sums[slot, t] + coef[o, MID] * cells[slot, t]
            if o:
                star += coef[o, TOUT] * cells[before, t] - coef[o, OUTER] * f_out[o - 1, t]
            if o + 1 < half:
                star = coef[o, ALPHA] * (star + coef[o, TIN] * cells[after, t])
            f_out[o, t] = star


def interface(w, g, sign, open_face, dz, dz_next):
    w = sign * w * open_face
    dz_min = jnp.minimum(dz, dz_next)
    g = g * open_face / (0.5 * (dz + dz_next))
    return dz_min * jnp.maximum(w, 0.0), dz_min * jnp.minimum(w, 0.0), g


def seam_kernel(nb, tc, count, star, cells, base, own, other, f_out, coef_out, message):
    half = nb * tc
    upper, _, _, _ = place(nb, tc)
    slot = jnp.where(upper == 1, 0, half - 1)
    sign, dz, dz_next = base[2], base[3], base[4]
    w = jnp.where(sign < 0.0, own[0], other[0])
    g = jnp.where(sign < 0.0, own[1], other[1])
    pos, neg, g = interface(w, g, sign, base[1], dz, dz_next)
    inner, outer_next = -g / dz, -g / dz_next
    mid, tout_next = neg / dz, -neg / dz_next
    alpha = 1.0 / (base[0] - inner)
    for t in range(count):
        c = cells[slot, t]
        f = alpha * (star[half - 1, t] + mid * c)
        f_out[t] = f
        message[t] = tout_next * c - outer_next * f
    coef_out[0] = inner * alpha
    coef_out[1] = alpha
    coef_out[2] = outer_next
    message[count] = alpha


def back_kernel(nb, tc, tpc, f_in, cin, f_last, coef, sent, got, *refs):
    half = nb * tc
    out, solved = refs[:-1], refs[-1]
    upper, rank, _, _ = place(nb, tc)
    slots = [jnp.where(upper == 1, half - 1 - o, o) for o in range(half)]
    other = coef[0] * got[tpc]
    scale = 1.0 / (1.0 - other * coef[2])
    mine, theirs = scale * coef[1], scale * other
    for t in range(tpc):
        x = f_last[t] + (mine * got[t] - theirs * sent[t])
        solved[slots[half - 1], t] = x
        for o in range(half - 2, -1, -1):
            x = f_in[o, t] - cin[o] * x
            solved[slots[o], t] = x
    for d, piece in zip(homeward(half), out):
        for t in range(tpc):
            piece[t] = solved[rank ^ d, t]


def join_kernel(nb, tc, tpc, *refs):
    half = nb * tc
    arrived, out, sem = refs[:half], refs[half], refs[half + 1]
    _, rank, _, _ = place(nb, tc)
    copies = []
    for d, piece in zip(homeward(half), arrived):
        r = rank ^ d
        cols = pl.ds(pl.multiple_of(lax.div(r, tc) * LANES, LANES), LANES)
        copies.append(
            pltpu.make_async_copy(
                piece, out.at[pl.ds(lax.rem(r, tc) * tpc, tpc), 0, :, cols], sem.at[d]
            )
        )
    for copy in copies:
        copy.start()
    for copy in copies:
        copy.wait()


def shards(tracer, east_flow, north_flow, up_flow, diffusivity, thickness, kmt, group, group_rate):
    ntr, ldev, ny, nx = tracer.shape
    count = lax.axis_size("lev")
    half = count // 2
    nb = nx // LANES
    tc = half // nb
    tpc = ntr // tc
    assert tc % 2 == 0 and 2 * tpc <= LANES
    assert ldev == 1 and ny == ROWS and nb * LANES == nx and tc * nb == half and tpc * tc == ntr
    tile = (ROWS, LANES)
    vm = pl.BlockSpec(memory_space=pltpu.VMEM)
    sm = pl.BlockSpec(memory_space=pltpu.SMEM)
    hbm = pl.BlockSpec(memory_space=pltpu.HBM)
    anywhere = pl.BlockSpec(memory_space=pl.ANY)
    params = pltpu.CompilerParams(vmem_limit_bytes=VMEM_LIMIT)

    def flip(value, bits):
        return lax.ppermute(value, "lev", [(i, i ^ bits) for i in range(count)])

    def struct(*shape):
        return jax.ShapeDtypeStruct(shape + tile, f32)

    def exchange(values, order):
        return [flip(piece, d) if d else piece for d, piece in zip(order, values)]

    packed = {}
    held = [
        pltpu.with_memory_space_constraint(value, pltpu.HBM)
        for value in (tracer, east_flow, north_flow, up_flow, diffusivity, kmt)
    ]
    ready = (
        pltpu.VMEM((half + 1,) + tile, f32),
        pltpu.VMEM((half + 1,) + tile, f32),
        pltpu.VMEM((tpc, half, LANES), f32),
    )
    for odd in range(2):
        distances = [d for d in devices(half) if d % 2 == odd]
        made = pl.pallas_call(
            functools.partial(pack_kernel, nb, tc, tpc, odd),
            out_shape=tuple(pltpu.VMEM((tpc + n_extra(d),) + tile, f32) for d in distances) + ready * odd,
            in_specs=[hbm] * 6 + [sm] * (3 * odd),
            out_specs=(vm,) * (len(distances) + 3 * odd),
            scratch_shapes=[
                pltpu.VMEM((ntr // 2, ny, nx), f32),
                pltpu.VMEM((4, ny, nx), f32),
                pltpu.VMEM((ny, nx), jnp.int32),
                pltpu.VMEM((tc // 2, nb) + tile, f32),
                pltpu.VMEM((group_rate.shape[0], half, LANES), f32),
                pltpu.SemaphoreType.DMA((5 + tc // 2,)),
                pltpu.SemaphoreType.DMA((half // 2,)),
            ],
            compiler_params=params,
            name="pack",
        )(*held, *(thickness, group, group_rate)[: 3 * odd])
        packed.update(zip(distances, made))
    wet, depth, decay = made[-3:]
    pieces = [packed[d] for d in devices(half)]
    arrived = exchange(pieces, devices(half))
    evens = half // 2 - 1
    relayed, seam = pl.pallas_call(
        functools.partial(relay_kernel, nb, tc, tpc),
        out_shape=(struct(4 * (evens + 1) + 2), struct(2)),
        in_specs=[vm] * (4 + evens),
        out_specs=(vm, vm),
        compiler_params=params,
        name="relay",
    )(east_flow, north_flow, up_flow, diffusivity, *arrived[:evens])
    swapped = flip(relayed, 1)
    own = pl.pallas_call(
        functools.partial(pick_kernel, nb, tc),
        out_shape=struct(2),
        in_specs=[vm, vm],
        out_specs=vm,
        compiler_params=params,
        name="pick",
    )(seam, swapped)
    other = flip(own, half)
    order = devices(half)
    cells, sums, coef, cin, base = pl.pallas_call(
        functools.partial(first_kernel, nb, tc, tpc),
        out_shape=(struct(half, tpc), struct(half, tpc), struct(half, 5), struct(half - 1), struct(5)),
        in_specs=[vm] * (4 + len(early(half))),
        out_specs=(vm,) * 5,
        scratch_shapes=[pltpu.VMEM((half, 2) + tile, f32)],
        compiler_params=params,
        name="first",
    )(wet, depth, decay, swapped, *[arrived[order.index(d)] for d in early(half)])
    late = [arrived[order.index(d)] for d in order if d not in early(half)]
    cells, _, f = pl.pallas_call(
        functools.partial(solve_kernel, nb, tc, tpc),
        out_shape=(struct(half, tpc), struct(half, tpc), struct(half, tpc)),
        in_specs=[vm] * (6 + len(late)),
        out_specs=(vm,) * 3,
        input_output_aliases={4 + len(late): 0, 5 + len(late): 1},
        compiler_params=params,
        name="solve",
    )(wet, decay, swapped, coef, *late, cells, sums)
    f_last, coef, message = pl.pallas_call(
        functools.partial(seam_kernel, nb, tc, tpc),
        out_shape=(struct(tpc), struct(3), struct(tpc + 1)),
        in_specs=[vm] * 5,
        out_specs=(vm,) * 3,
        compiler_params=params,
        name="seam",
    )(f, cells, base, own, other)
    solved = pl.pallas_call(
        functools.partial(back_kernel, nb, tc, tpc),
        out_shape=(struct(tpc),) * half,
        in_specs=[vm] * 6,
        out_specs=(vm,) * half,
        scratch_shapes=[pltpu.VMEM((half, tpc) + tile, f32)],
        compiler_params=params,
        name="back",
    )(f, cin, f_last, coef, message, flip(message, half))
    back = exchange(solved, homeward(half))
    return pl.pallas_call(
        functools.partial(join_kernel, nb, tc, tpc),
        out_shape=jax.ShapeDtypeStruct(tracer.shape, f32),
        in_specs=[anywhere] * len(back),
        out_specs=hbm,
        scratch_shapes=[pltpu.SemaphoreType.DMA((half,))],
        compiler_params=params,
        name="join",
    )(*back)


def solution(mesh):
    placed = (
        P(None, "lev", "band", None),
        P("lev", "band", None),
        P("lev", "band", None),
        P("lev", "band", None),
        P("lev", "band", None),
        P(),
        P("band", None),
        P(),
        P(),
    )
    return jax.shard_map(
        shards, mesh=mesh, in_specs=placed, out_specs=P(None, "lev", "band", None), check_vma=False
    )
```

```python
import functools

import jax
import jax.numpy as jnp
from jax import lax
from jax.experimental import pallas as pl
from jax.experimental.pallas import tpu as pltpu
from jax.sharding import PartitionSpec as P

LANES = 128
ROWS = 8
MID, TOUT, TIN, OUTER, ALPHA = range(5)
EDGE, EAST, NORTH, UP, DIFF, EXTRA = 0, 1, 2, 3, 4, 5
f32 = jnp.float32
VMEM_LIMIT = 16 * 1024 * 1024


def lanes_iota():
    return lax.broadcasted_iota(jnp.int32, (ROWS, LANES), 1)


def rows_iota():
    return lax.broadcasted_iota(jnp.int32, (ROWS, LANES), 0)


def crossed(half, d):
    return (d & half // 2 > 0) + (d & half // 4 > 0)


def devices(half):
    return sorted(range(1, half), key=lambda d: (d < 2, d & 1, -crossed(half, d), -d)) + [0]


def homeward(half):
    return sorted(range(1, half), key=lambda d: (d < 2, d & 1, -crossed(half, d), d)) + [0]


def early(half):
    return [d for d in devices(half) if d < 2 or d % 2 == 0 or crossed(half, d) == 2]


def n_extra(d):
    return 1 if d % 2 else EXTRA


def place(nb, tc):
    half = nb * tc
    index = lax.axis_index("lev")
    rank = lax.rem(index, half)
    return lax.div(index, half), rank, lax.div(rank, tc), lax.rem(rank, tc)


def pack_kernel(nb, tc, tpc, odd, tracer, east, north, up, diff, kmt, *refs):
    half = nb * tc
    _, rank, _, chunk = place(nb, tc)
    distances = [d for d in devices(half) if d % 2 == odd]
    turns = range(odd, tc, 2)
    scalars, refs = refs[: 3 * odd], refs[3 * odd :]
    out, ready = dict(zip(distances, refs)), refs[len(distances) : -7]
    cells, fields, depth, extra, table, sem, store_sem = refs[-7:]
    loads = [pltpu.make_async_copy(kmt, depth, sem.at[0])]
    for i, field in enumerate((east,) if odd else (east, north, up, diff)):
        loads.append(pltpu.make_async_copy(field, fields.at[pl.ds(i, 1)], sem.at[1 + i]))
    chunks = [
        pltpu.make_async_copy(
            tracer.at[pl.ds((chunk ^ e) * tpc, tpc), 0], cells.at[pl.ds(e // 2 * tpc, tpc)], sem.at[5 + e // 2]
        )
        for e in turns
    ]
    for copy in chunks + loads:
        copy.start()
    stores = []
    for d in distances:
        cut = pl.ds(pl.multiple_of(lax.div(rank ^ d, tc) * LANES, LANES), LANES)
        copy = pltpu.make_async_copy(
            tracer.at[pl.ds((chunk ^ d % tc) * tpc, tpc), 0, :, cut], out[d].at[pl.ds(0, tpc)], store_sem.at[d // 2]
        )
        copy.start()
        stores.append(copy)
    for copy in loads:
        copy.wait()
    if odd:
        prepare(nb, tc, tpc, *scalars, depth, *ready, table)
    for copy in chunks:
        copy.wait()
    lane = lanes_iota()
    cols = [slice(b * LANES, (b + 1) * LANES) for b in range(nb)]
    wet = [(lax.axis_index("lev") < depth[:, cols[b]]).astype(f32) for b in range(nb)]
    flow = [None]
    for b in range(1, nb):
        ends = fields[0, :, cols[b - 1]][:, LANES - 1 :]
        ends = ends * wet[b - 1][:, LANES - 1 :] * wet[b][:, :1]
        flow.append(jnp.broadcast_to(ends, (ROWS, LANES)))
    for e in turns:
        faces = [jnp.zeros((ROWS, LANES), f32) for _ in range(nb)]
        for t in range(tpc):
            at = e // 2 * tpc + t
            for b in range(1, nb):
                west = pltpu.roll(cells[at, :, cols[b - 1]], (2 * t + 1) % LANES, 1)
                here = cells[at, :, cols[b]]
                here = pltpu.roll(here, 2 * t, 1) if t else here
                face = jnp.maximum(flow[b], 0.0) * west + jnp.minimum(flow[b], 0.0) * here
                faces[b] = jnp.where(lane == 2 * t, face, faces[b])
        for b in range(nb):
            edge = faces[b]
            if b + 1 < nb:
                edge = edge - pltpu.roll(faces[b + 1], LANES - 1, 1)
            extra[e // 2, b] = edge
    for d in distances:
        block = lax.div(rank ^ d, tc)
        cut = pl.ds(pl.multiple_of(block * LANES, LANES), LANES)
        out[d][tpc + EDGE] = extra[d % tc // 2, block]
        if not odd:
            for i in range(4):
                out[d][tpc + EAST + i] = fields[i, :, cut]
    for copy in stores:
        copy.wait()


def relay_kernel(nb, tc, tpc, east, north, up, diff, *refs):
    half = nb * tc
    arrived, (out, seam) = refs[:-2], refs[-2:]
    _, rank, block, _ = place(nb, tc)
    cols = pl.ds(pl.multiple_of(block * LANES, LANES), LANES)
    for j, even in enumerate(arrived):
        for i in range(4):
            out[4 * j + i] = even[tpc + EAST + i]
    own = [level[0, :, cols] for level in (east, north, up, diff)]
    for i in range(4):
        out[4 * len(arrived) + i] = own[i]
    for i in range(2):
        field = own[UP - EAST + i]
        for d, even in zip(devices(half), arrived):
            field = jnp.where(rank == d, even[tpc + UP + i], field)
        out[4 * len(arrived) + 4 + i] = field
        seam[i] = field


def pick_kernel(nb, tc, seam, swapped, own):
    _, rank, _, _ = place(nb, tc)
    for i in range(2):
        own[i] = jnp.where(lax.rem(rank, 2) == 1, swapped[swapped.shape[0] - 2 + i], seam[i])


def prepare(nb, tc, tpc, thickness, group, rates, kmt_all, wet, depth, decay, table):
    half = nb * tc
    upper, _, block, chunk = place(nb, tc)
    kmt = kmt_all[:, pl.ds(pl.multiple_of(block * LANES, LANES), LANES)]
    levels = [jnp.where(upper == 1, 2 * half - 1 - o, o) for o in range(half + 1)]
    for o, k in enumerate(levels):
        wet[o] = (k < kmt).astype(f32)
        depth[o] = jnp.full((ROWS, LANES), thickness[k], f32)
    row = rows_iota()
    for g in range(rates.shape[0]):
        for at in range(0, half, ROWS):
            tile = jnp.zeros((ROWS, LANES), f32)
            for i in range(min(ROWS, half - at)):
                tile = jnp.where(row == i, rates[g, levels[at + i]], tile)
            table[g, at : at + ROWS] = tile[: min(ROWS, half - at)]
    for t in range(tpc):
        decay[t] = table[group[chunk * tpc + t]]


def horizontal(half, tpc, d, piece, fields, rank, upper, wets, decay, cells, sums):
    lane, row = lanes_iota(), rows_iota()
    ends = jnp.logical_or(lane == 0, lane == LANES - 1)
    slot = rank ^ d
    o = jnp.where(upper == 1, half - 1 - slot, slot)
    wet = wets[o]
    east = fields[0] * wet * pltpu.roll(wet, LANES - 1, 1)
    east = jnp.where(lane == LANES - 1, 0.0, east)
    north = fields[1] * wet * pltpu.roll(wet, ROWS - 1, 0)
    north = jnp.where(row == ROWS - 1, 0.0, north)
    e_pos, e_neg = jnp.maximum(east, 0.0), jnp.minimum(east, 0.0)
    n_pos, n_neg = jnp.maximum(north, 0.0), jnp.minimum(north, 0.0)
    mid = wet - e_pos - n_pos + pltpu.roll(e_neg, 1, 1) + pltpu.roll(n_neg, 1, 0)
    e_pos, n_pos = pltpu.roll(e_pos, 1, 1), pltpu.roll(n_pos, 1, 0)
    edges = piece[tpc + EDGE]
    for t in range(tpc):
        c = piece[t]
        star = c * (mid - decay[t, pl.ds(o, 1)] * wet)
        star += e_pos * pltpu.roll(c, 1, 1) - e_neg * pltpu.roll(c, LANES - 1, 1)
        star += n_pos * pltpu.roll(c, 1, 0) - n_neg * pltpu.roll(c, ROWS - 1, 0)
        edge = pltpu.roll(edges, LANES - 2 * t, 1) if t else edges
        cells[slot, t] = c
        sums[slot, t] = star + jnp.where(ends, edge, 0.0)


def field_of(half, tpc, d, pieces, swapped):
    evens = [e for e in devices(half) if e % 2 == 0]
    if d % 2 == 0:
        return [pieces[d][tpc + EAST + i] for i in range(4)]
    return [swapped[4 * evens.index(d ^ 1) + i] for i in range(4)]


def first_kernel(nb, tc, tpc, wets, depths, decay, swapped, *refs):
    half = nb * tc
    pieces = dict(zip(early(half), refs))
    cells, sums, coef, cin_out, base, vertical = refs[len(pieces) :]
    upper, rank, _, _ = place(nb, tc)
    sign = 1.0 - 2.0 * upper.astype(f32)
    for d in range(half):
        fields = field_of(half, tpc, d, pieces, swapped)
        vertical[rank ^ d, 0], vertical[rank ^ d, 1] = fields[2], fields[3]
        if d in pieces:
            horizontal(half, tpc, d, pieces[d], fields, rank, upper, wets, decay, cells, sums)

    def slot_of(o):
        return jnp.where(upper == 1, half - 1 - o, o)

    zero = jnp.zeros((ROWS, LANES), f32)
    cin = tout = outer = mid = zero
    for o in range(half):
        dz, dz_next = depths[o], depths[o + 1]
        open_face = wets[o] * wets[o + 1]
        denom = 1.0 - outer - outer * cin
        coef[o, TOUT], coef[o, OUTER] = tout, outer
        if o + 1 == half:
            coef[o, MID] = mid
            base[0], base[1], base[3], base[4] = denom, open_face, dz, dz_next
            base[2] = jnp.full((ROWS, LANES), sign, f32)
        else:
            face = jnp.where(upper == 1, slot_of(o), slot_of(o + 1))
            pos, neg, g = interface(vertical[face, 0], vertical[face, 1], sign, open_face, dz, dz_next)
            inner = -g / dz
            alpha = 1.0 / (denom - inner)
            cin = inner * alpha
            coef[o, MID], coef[o, TIN], coef[o, ALPHA] = mid + neg / dz, pos / dz, alpha
            cin_out[o] = cin
            tout, outer, mid = -neg / dz_next, -g / dz_next, -pos / dz_next


def solve_kernel(nb, tc, tpc, wets, decay, swapped, coef, *refs):
    half = nb * tc
    late = [d for d in devices(half) if d not in early(half)]
    pieces = dict(zip(late, refs))
    cells, sums, f_out = refs[-3:]
    upper, rank, _, _ = place(nb, tc)
    for d in late:
        fields = field_of(half, tpc, d, pieces, swapped)
        horizontal(half, tpc, d, pieces[d], fields, rank, upper, wets, decay, cells, sums)
    for o in range(half):
        slot, before, after = [jnp.where(upper == 1, half - 1 - k, k) for k in (o, o - 1, o + 1)]
        for t in range(tpc):
            star = sums[slot, t] + coef[o, MID] * cells[slot, t]
            if o:
                star += coef[o, TOUT] * cells[before, t] - coef[o, OUTER] * f_out[o - 1, t]
            if o + 1 < half:
                star = coef[o, ALPHA] * (star + coef[o, TIN] * cells[after, t])
            f_out[o, t] = star


def interface(w, g, sign, open_face, dz, dz_next):
    w = sign * w * open_face
    dz_min = jnp.minimum(dz, dz_next)
    g = g * open_face / (0.5 * (dz + dz_next))
    return dz_min * jnp.maximum(w, 0.0), dz_min * jnp.minimum(w, 0.0), g


def seam_kernel(nb, tc, count, star, cells, base, own, other, f_out, coef_out, message):
    half = nb * tc
    upper, _, _, _ = place(nb, tc)
    slot = jnp.where(upper == 1, 0, half - 1)
    sign, dz, dz_next = base[2], base[3], base[4]
    w = jnp.where(sign < 0.0, own[0], other[0])
    g = jnp.where(sign < 0.0, own[1], other[1])
    pos, neg, g = interface(w, g, sign, base[1], dz, dz_next)
    inner, outer_next = -g / dz, -g / dz_next
    mid, tout_next = neg / dz, -neg / dz_next
    alpha = 1.0 / (base[0] - inner)
    for t in range(count):
        c = cells[slot, t]
        f = alpha * (star[half - 1, t] + mid * c)
        f_out[t] = f
        message[t] = tout_next * c - outer_next * f
    coef_out[0] = inner * alpha
    coef_out[1] = alpha
    coef_out[2] = outer_next
    message[count] = alpha


def back_kernel(nb, tc, tpc, f_in, cin, f_last, coef, sent, got, *refs):
    half = nb * tc
    out, solved = refs[:-1], refs[-1]
    upper, rank, _, _ = place(nb, tc)
    slots = [jnp.where(upper == 1, half - 1 - o, o) for o in range(half)]
    other = coef[0] * got[tpc]
    scale = 1.0 / (1.0 - other * coef[2])
    mine, theirs = scale * coef[1], scale * other
    for t in range(tpc):
        x = f_last[t] + (mine * got[t] - theirs * sent[t])
        solved[slots[half - 1], t] = x
        for o in range(half - 2, -1, -1):
            x = f_in[o, t] - cin[o] * x
            solved[slots[o], t] = x
    for d, piece in zip(homeward(half), out):
        for t in range(tpc):
            piece[t] = solved[rank ^ d, t]


def join_kernel(nb, tc, tpc, *refs):
    half = nb * tc
    arrived, out, sem = refs[:half], refs[half], refs[half + 1]
    _, rank, _, _ = place(nb, tc)
    copies = []
    for d, piece in zip(homeward(half), arrived):
        r = rank ^ d
        cols = pl.ds(pl.multiple_of(lax.div(r, tc) * LANES, LANES), LANES)
        copies.append(
            pltpu.make_async_copy(
                piece, out.at[pl.ds(lax.rem(r, tc) * tpc, tpc), 0, :, cols], sem.at[d]
            )
        )
    for copy in copies:
        copy.start()
    for copy in copies:
        copy.wait()


def shards(tracer, east_flow, north_flow, up_flow, diffusivity, thickness, kmt, group, group_rate):
    ntr, ldev, ny, nx = tracer.shape
    count = lax.axis_size("lev")
    half = count // 2
    nb = nx // LANES
    tc = half // nb
    tpc = ntr // tc
    assert tc % 2 == 0 and 2 * tpc <= LANES
    assert ldev == 1 and ny == ROWS and nb * LANES == nx and tc * nb == half and tpc * tc == ntr
    tile = (ROWS, LANES)
    vm = pl.BlockSpec(memory_space=pltpu.VMEM)
    sm = pl.BlockSpec(memory_space=pltpu.SMEM)
    hbm = pl.BlockSpec(memory_space=pltpu.HBM)
    anywhere = pl.BlockSpec(memory_space=pl.ANY)
    params = pltpu.CompilerParams(vmem_limit_bytes=VMEM_LIMIT)

    def flip(value, bits):
        return lax.ppermute(value, "lev", [(i, i ^ bits) for i in range(count)])

    def struct(*shape):
        return jax.ShapeDtypeStruct(shape + tile, f32)

    def exchange(values, order):
        return [flip(piece, d) if d else piece for d, piece in zip(order, values)]

    packed = {}
    held = [
        pltpu.with_memory_space_constraint(value, pltpu.HBM)
        for value in (tracer, east_flow, north_flow, up_flow, diffusivity, kmt)
    ]
    ready = (
        pltpu.VMEM((half + 1,) + tile, f32),
        pltpu.VMEM((half + 1,) + tile, f32),
        pltpu.VMEM((tpc, half, LANES), f32),
    )
    for odd in range(2):
        distances = [d for d in devices(half) if d % 2 == odd]
        made = pl.pallas_call(
            functools.partial(pack_kernel, nb, tc, tpc, odd),
            out_shape=tuple(pltpu.VMEM((tpc + n_extra(d),) + tile, f32) for d in distances) + ready * odd,
            in_specs=[hbm] * 6 + [sm] * (3 * odd),
            out_specs=(vm,) * (len(distances) + 3 * odd),
            scratch_shapes=[
                pltpu.VMEM((ntr // 2, ny, nx), f32),
                pltpu.VMEM((4, ny, nx), f32),
                pltpu.VMEM((ny, nx), jnp.int32),
                pltpu.VMEM((tc // 2, nb) + tile, f32),
                pltpu.VMEM((group_rate.shape[0], half, LANES), f32),
                pltpu.SemaphoreType.DMA((5 + tc // 2,)),
                pltpu.SemaphoreType.DMA((half // 2,)),
            ],
            compiler_params=params,
            name="pack",
        )(*held, *(thickness, group, group_rate)[: 3 * odd])
        packed.update(zip(distances, made))
    wet, depth, decay = made[-3:]
    pieces = [packed[d] for d in devices(half)]
    arrived = exchange(pieces, devices(half))
    evens = half // 2 - 1
    relayed, seam = pl.pallas_call(
        functools.partial(relay_kernel, nb, tc, tpc),
        out_shape=(struct(4 * (evens + 1) + 2), struct(2)),
        in_specs=[vm] * (4 + evens),
        out_specs=(vm, vm),
        compiler_params=params,
        name="relay",
    )(east_flow, north_flow, up_flow, diffusivity, *arrived[:evens])
    swapped = flip(relayed, 1)
    own = pl.pallas_call(
        functools.partial(pick_kernel, nb, tc),
        out_shape=struct(2),
        in_specs=[vm, vm],
        out_specs=vm,
        compiler_params=params,
        name="pick",
    )(seam, swapped)
    other = flip(own, half)
    order = devices(half)
    cells, sums, coef, cin, base = pl.pallas_call(
        functools.partial(first_kernel, nb, tc, tpc),
        out_shape=(struct(half, tpc), struct(half, tpc), struct(half, 5), struct(half - 1), struct(5)),
        in_specs=[vm] * (4 + len(early(half))),
        out_specs=(vm,) * 5,
        scratch_shapes=[pltpu.VMEM((half, 2) + tile, f32)],
        compiler_params=params,
        name="first",
    )(wet, depth, decay, swapped, *[arrived[order.index(d)] for d in early(half)])
    late = [arrived[order.index(d)] for d in order if d not in early(half)]
    cells, _, f = pl.pallas_call(
        functools.partial(solve_kernel, nb, tc, tpc),
        out_shape=(struct(half, tpc), struct(half, tpc), struct(half, tpc)),
        in_specs=[vm] * (6 + len(late)),
        out_specs=(vm,) * 3,
        input_output_aliases={4 + len(late): 0, 5 + len(late): 1},
        compiler_params=params,
        name="solve",
    )(wet, decay, swapped, coef, *late, cells, sums)
    f_last, coef, message = pl.pallas_call(
        functools.partial(seam_kernel, nb, tc, tpc),
        out_shape=(struct(tpc), struct(3), struct(tpc + 1)),
        in_specs=[vm] * 5,
        out_specs=(vm,) * 3,
        compiler_params=params,
        name="seam",
    )(f, cells, base, own, other)
    solved = pl.pallas_call(
        functools.partial(back_kernel, nb, tc, tpc),
        out_shape=(struct(tpc),) * half,
        in_specs=[vm] * 6,
        out_specs=(vm,) * half,
        scratch_shapes=[pltpu.VMEM((half, tpc) + tile, f32)],
        compiler_params=params,
        name="back",
    )(f, cin, f_last, coef, message, flip(message, half))
    back = exchange(solved, homeward(half))
    return pl.pallas_call(
        functools.partial(join_kernel, nb, tc, tpc),
        out_shape=jax.ShapeDtypeStruct(tracer.shape, f32),
        in_specs=[anywhere] * len(back),
        out_specs=hbm,
        scratch_shapes=[pltpu.SemaphoreType.DMA((half,))],
        compiler_params=params,
        name="join",
    )(*back)


def solution(mesh):
    placed = (
        P(None, "lev", "band", None),
        P("lev", "band", None),
        P("lev", "band", None),
        P("lev", "band", None),
        P("lev", "band", None),
        P(),
        P("band", None),
        P(),
        P(),
    )
    return jax.shard_map(
        shards, mesh=mesh, in_specs=placed, out_specs=P(None, "lev", "band", None), check_vma=False
    )
```
